256 devices in a mesh: section: 4 (over x), seq: 64 (over z, y, core).
Axes of the slice: x: 4, y: 4, z: 8, core: 2. Of those that a mesh axis runs over, the one named last changes fastest.
Arguments:
- patches: bfloat16 [2, 4096, 2048], P(None, 'seq'), may hold values from -6 to 6
- stale_cache: bfloat16 [4, 2, 4096, 4096], P('section', None, 'seq'), may hold values from -200 to 200
- block_lists: int32 [4, 16, 512, 16], P('section'), may hold values from 0 to 255, as said below
- block_counts: int32 [4, 16], P('section'), may hold values from 8 to 16, as said below
- query_gain: float32 [4, 2048], P('section'), may hold values from 1 to 3
- branch_gate: float32 [4, 2048], P('section'), may hold values from 1 to 4
Outputs:
- section_outputs: bfloat16 [4, 2, 4096, 2048], P('section', None, 'seq')
The draws below stay inside these ranges and needn't reach their ends.
Inputs may be any that keep to these rules, and one draw needn't show every extreme that they name: `block_lists`: for each section, head and query block the 16 entries are distinct key block numbers; the first is the key block that holds the query block's own tokens. `block_counts`: all query blocks of one head in one section use the same number of list entries; in every section some head uses 16.
All inputs are finite; a program needn't handle non-finite values.
Results may differ from the reference program's by a relative error of at most 0.02.
The reference program's roundings to bfloat16 on the way count: a program that leaves them out, or rounds other values in their place, can miss the bound.
Values may be sent and summed in bfloat16 or wider, within the bound.
No kernel may reach another device: no remote copies, remote signals or barrier semaphores. Data moves between devices by JAX's collectives and lax.ppermute only.
A program may use at most 128 MiB of HBM per device.

```python
import math
import jax
import jax.numpy as jnp
from jax import lax

HEADS = 16
HEAD_DIM = 128
CHANNELS = 2048
MICRO = 2
QUERY_BLOCK = 16
KEY_BLOCK = 32
SLOTS = 16
PATCH_TOKENS = 4096
ALL_TOKENS = 8192
QUERY_BLOCKS = 512
KEY_BLOCKS = 256
N_SECTION = 4


def draw_stale_cache(key, part):
    full_shape = (N_SECTION, MICRO, PATCH_TOKENS, 2, HEADS, HEAD_DIM)
    key_base = jax.random.fold_in(key, 0)
    values = jnp.clip(jax.random.normal(key_base, full_shape, jnp.float32), -6.0, 6.0)
    return values.reshape(N_SECTION, MICRO, PATCH_TOKENS, 2 * HEADS * HEAD_DIM).astype(jnp.bfloat16)


def draw_block_lists(key, part):
    ranking = jax.random.randint(key, (N_SECTION, HEADS, QUERY_BLOCKS, KEY_BLOCKS), 0, 2 ** 20) * KEY_BLOCKS
    ranking = ranking + jnp.arange(KEY_BLOCKS, dtype=jnp.int32)
    own_block = jnp.arange(QUERY_BLOCKS, dtype=jnp.int32) * QUERY_BLOCK // KEY_BLOCK
    ranking = jnp.where(jnp.arange(KEY_BLOCKS, dtype=jnp.int32)[None, :] == own_block[:, None], 2 ** 30, ranking)
    return lax.top_k(ranking, SLOTS)[1].astype(jnp.int32)


def draw_block_counts(key, part):
    key_count, key_full = jax.random.split(key)
    count_draw = jax.random.randint(key_count, (N_SECTION, HEADS), SLOTS // 2, SLOTS + 1)
    fullest = jax.random.randint(key_full, (N_SECTION, 1), 0, HEADS)
    return jnp.where(jnp.arange(HEADS)[None, :] == fullest, SLOTS, count_draw).astype(jnp.int32)


def steps_of(key, dims, cuts, low, largest):
    factor_of = 1.0
    for position, blocks in cuts:
        heights = jax.random.uniform(jax.random.fold_in(jax.random.fold_in(key, 6), position), (blocks,), jnp.float32, low / len(cuts), largest / len(cuts))
        factor_of = factor_of * jnp.repeat(jnp.exp(heights), dims[position] // blocks).reshape((-1,) + (1,) * (len(dims) - 1 - position))
    return factor_of


def centred(rng, dims, deviation, reach, cuts=(), kind=jnp.bfloat16):
    gain = steps_of(rng, dims, cuts, -0.22, 0.18) if cuts else 1.0
    values = jax.random.normal(rng, dims, jnp.float32) * deviation * gain
    return jnp.minimum(jnp.maximum(values, -reach), reach).astype(kind)


def setup_inputs(seed: int = 0) -> dict:
    streams_of = jax.random.split(jax.random.key(seed), 7)
    patches = centred(streams_of[0], (MICRO, PATCH_TOKENS, CHANNELS), 1.0, 6.0, ((1, 64),))
    stale_cache = draw_stale_cache(jax.random.fold_in(streams_of[6], 71), 0)
    block_lists = draw_block_lists(jax.random.fold_in(streams_of[6], 71), 0)
    block_counts = draw_block_counts(jax.random.fold_in(streams_of[6], 71), 0)
    query_gain = jnp.clip(jnp.exp(math.log(3.0) - 1.0986123 * jax.random.uniform(streams_of[4], (N_SECTION, CHANNELS), jnp.float32) ** steps_of(streams_of[4], (N_SECTION, CHANNELS), ((0, 4),), -0.2, 0.2)), 1.0, 3.0)
    branch_gate = jnp.clip(jnp.exp(math.log(4.0) - 1.3862944 * jax.random.uniform(streams_of[5], (N_SECTION, CHANNELS), jnp.float32) ** steps_of(streams_of[5], (N_SECTION, CHANNELS), ((0, 4),), -0.2, 0.2)), 1.0, 4.0)
    return dict(patches=patches, stale_cache=stale_cache, block_lists=block_lists, block_counts=block_counts, query_gain=query_gain, branch_gate=branch_gate)


SCORE_FLOOR = -1e+30

def attend(queries, blocks, positions, count):
    n_query, q_rows, head_width = queries.shape
    slot_total = positions.shape[1]
    block_rows = blocks.shape[1]
    group_size = math.gcd(n_query, 16)
    query_groups = queries.reshape(n_query // group_size, group_size, q_rows, head_width)
    position_groups = positions.reshape(n_query // group_size, group_size, slot_total)
    slot_live = jnp.arange(slot_total * block_rows) // block_rows < count
    scale_factor = head_width ** (-0.5)

    def one_group(group_pair):
        query_part, position_part = group_pair
        picked = jnp.take(blocks, position_part, axis=0)
        keys_part = picked[..., :head_width].reshape(group_size, slot_total * block_rows, head_width)
        value_part = picked[..., head_width:].reshape(group_size, slot_total * block_rows, head_width)
        query_wide = lax.optimization_barrier(query_part).astype(jnp.float32)
        scores = jnp.einsum('gqd,gkd->gqk', query_wide, keys_part.astype(jnp.float32)) * scale_factor
        scores = jnp.where(slot_live, scores, SCORE_FLOOR)
        highest = lax.optimization_barrier(jnp.max(scores, axis=-1, keepdims=True))
        exponent = jnp.exp(scores - highest)
        weights = (exponent / lax.optimization_barrier(jnp.sum(exponent, axis=-1, keepdims=True))).astype(jnp.bfloat16)
        weights = lax.optimization_barrier(weights).astype(jnp.float32)
        summed = jnp.einsum('gqk,gkd->gqd', weights, value_part.astype(jnp.float32))
        return summed.astype(jnp.bfloat16)
    result = lax.map(one_group, (query_groups, position_groups))
    return result.reshape(n_query, q_rows, head_width)

def reference(patches, stale_cache, block_lists, block_counts, query_gain, branch_gate):
    section_results = []
    current_list = [patches[micro_index] for micro_index in range(MICRO)]
    blocks_per_micro = PATCH_TOKENS // QUERY_BLOCK
    for section_number in range(N_SECTION):
        cache_rows = stale_cache[section_number].reshape(ALL_TOKENS, 2, HEADS, HEAD_DIM)
        head_blocks = cache_rows.transpose(2, 0, 1, 3).reshape(HEADS, KEY_BLOCKS, KEY_BLOCK, 2 * HEAD_DIM)
        head_gain = query_gain[section_number].reshape(HEADS, HEAD_DIM)
        section_rows = []
        for micro_index in range(MICRO):
            widened = current_list[micro_index].astype(jnp.float32)
            per_head = widened.reshape(PATCH_TOKENS, HEADS, HEAD_DIM)
            normed = per_head * lax.rsqrt(lax.optimization_barrier(jnp.mean(per_head * per_head, axis=-1, keepdims=True)) + 1e-06) * head_gain
            queries = normed.astype(jnp.bfloat16).transpose(1, 0, 2).reshape(HEADS, blocks_per_micro, QUERY_BLOCK, HEAD_DIM)
            start_block = micro_index * blocks_per_micro
            lists_now = block_lists[section_number, :, start_block:start_block + blocks_per_micro]

            def one_head(bundle):
                head_queries, head_cache, head_lists, head_count = bundle
                return attend(head_queries, head_cache, head_lists, head_count)
            outputs = lax.map(one_head, (queries, head_blocks, lists_now, block_counts[section_number]))
            merged = outputs.reshape(HEADS, PATCH_TOKENS, HEAD_DIM).transpose(1, 0, 2).reshape(PATCH_TOKENS, CHANNELS)
            merged = lax.optimization_barrier(merged).astype(jnp.float32)
            updated = (widened + branch_gate[section_number] * merged).astype(jnp.bfloat16)
            section_rows.append(updated)
        section_results.append(jnp.stack(section_rows))
        current_list = section_rows
    return jnp.stack(section_results)
```

```python
import functools

import jax
import jax.numpy as jnp
from jax import lax
from jax.experimental import pallas as pl
from jax.experimental.pallas import tpu as pltpu
from jax.sharding import Mesh, PartitionSpec as P

HEADS = 16
HEAD_DIM = 128
QUERY_BLOCK = 16
KEY_BLOCK = 32
SLOTS = 16
SECTIONS = 4
CHUNKS = 4
GROUP = 8
SPAN = SLOTS * KEY_BLOCK
SCORE_FLOOR = -1e30

OWNERS = ("z", "yh")


def attend_kernel(
    places, meta, x_ref, gain_ref, gate_ref, *rest, pieces, groups
):
    k_parts = rest[:pieces]
    v_parts = rest[pieces : 2 * pieces]
    out_ref, k_tab, v_tab, sems = rest[2 * pieces :]
    rows = k_tab.shape[0] // pieces
    base = meta[1]
    live_keys = meta[2] * KEY_BLOCK

    @pl.when(meta[0] > 0)
    def _():
        copies = []
        for which, (parts, tab) in enumerate(((k_parts, k_tab), (v_parts, v_tab))):
            for p in range(pieces):
                copy = pltpu.make_async_copy(
                    parts[p], tab.at[pl.ds(p * rows, rows), :], sems.at[which, p]
                )
                copy.start()
                copies.append(copy)
        for copy in copies:
            copy.wait()

        def one_group(index, carry):
            row0 = pl.multiple_of(index * (GROUP * QUERY_BLOCK), GROUP * QUERY_BLOCK)
            wide = x_ref[pl.ds(row0, GROUP * QUERY_BLOCK), :].astype(jnp.float32)
            mean = jnp.mean(wide * wide, axis=-1, keepdims=True)
            queries = (wide * lax.rsqrt(mean + 1e-06) * gain_ref[...]).astype(jnp.bfloat16)
            first = base + index * (GROUP * SLOTS)
            scores = []
            starts = []
            for g in range(GROUP):
                at = [
                    pl.multiple_of(places[first + g * SLOTS + j], KEY_BLOCK)
                    for j in range(SLOTS)
                ]
                starts.append(at)
                keys = jnp.concatenate(
                    [k_tab[pl.ds(a, KEY_BLOCK), :] for a in at], axis=0
                )
                scores.append(
                    lax.dot_general(
                        queries[g * QUERY_BLOCK : (g + 1) * QUERY_BLOCK],
                        keys,
                        (((1,), (1,)), ((), ())),
                        preferred_element_type=jnp.float32,
                    )
                )
            scores = jnp.concatenate(scores, axis=0) * (HEAD_DIM**-0.5)
            lane = lax.broadcasted_iota(jnp.int32, scores.shape, 1)
            scores = jnp.where(lane < live_keys, scores, SCORE_FLOOR)
            highest = jnp.max(scores, axis=-1, keepdims=True)
            exponent = jnp.exp(scores - highest)
            total = jnp.sum(exponent, axis=-1, keepdims=True)
            weights = (exponent / total).astype(jnp.bfloat16)
            summed = []
            for g in range(GROUP):
                values = jnp.concatenate(
                    [v_tab[pl.ds(a, KEY_BLOCK), :] for a in starts[g]], axis=0
                )
                summed.append(
                    jnp.dot(
                        weights[g * QUERY_BLOCK : (g + 1) * QUERY_BLOCK],
                        values,
                        preferred_element_type=jnp.float32,
                    )
                )
            heads = jnp.concatenate(summed, axis=0).astype(jnp.bfloat16)
            updated = wide + gate_ref[...] * heads.astype(jnp.float32)
            out_ref[pl.ds(row0, GROUP * QUERY_BLOCK), :] = updated.astype(jnp.bfloat16)
            return carry

        lax.fori_loop(0, groups, one_group, 0)

    @pl.when(meta[0] <= 0)
    def _():
        out_ref[...] = jnp.zeros_like(out_ref)


def attend(places, meta, x, gain, gate, k_parts, v_parts):
    pieces = len(k_parts)
    rows = k_parts[0].shape[0]
    total = pieces * rows
    queries = x.shape[0]
    vmem = pl.BlockSpec(memory_space=pltpu.VMEM)
    smem = pl.BlockSpec(memory_space=pltpu.SMEM)
    hbm = pl.BlockSpec(memory_space=pl.ANY)
    return pl.pallas_call(
        functools.partial(
            attend_kernel, pieces=pieces, groups=queries // (GROUP * QUERY_BLOCK)
        ),
        out_shape=jax.ShapeDtypeStruct(x.shape, jnp.bfloat16),
        in_specs=[smem, smem, vmem, vmem, vmem] + [hbm] * (2 * pieces),
        out_specs=vmem,
        scratch_shapes=[
            pltpu.VMEM((total, HEAD_DIM), jnp.bfloat16),
            pltpu.VMEM((total, HEAD_DIM), jnp.bfloat16),
            pltpu.SemaphoreType.DMA((2, pieces)),
        ],
        compiler_params=pltpu.CompilerParams(vmem_limit_bytes=24 * 1024 * 1024),
        cost_estimate=pl.CostEstimate(
            flops=4 * queries * SPAN * HEAD_DIM,
            bytes_accessed=2 * total * HEAD_DIM * 2,
            transcendentals=queries * SPAN,
        ),
    )(places, meta, x, gain, gate, *k_parts, *v_parts)


def swapped(value, axis):
    return lax.ppermute(value, axis, [(0, 1), (1, 0)])


def spread(value):
    other = swapped(value, "yl")
    return [value, other, swapped(value, "core"), swapped(other, "core")]


def local(patches, stale_cache, block_lists, block_counts, query_gain, branch_gate):
    section = lax.axis_index("section")
    owner = lax.axis_index("z") * lax.axis_size("yh") + lax.axis_index("yh")
    yl, core = lax.axis_index("yl"), lax.axis_index("core")
    micro_count, patch_rows, channels = patches.shape
    sources = lax.axis_size("z") * lax.axis_size("yh")
    tokens = micro_count * patch_rows
    chunk_tokens = tokens // CHUNKS

    by_head = stale_cache[0].reshape(tokens, 2, HEADS, HEAD_DIM).transpose(1, 2, 0, 3)
    mine = lax.dynamic_slice_in_dim(
        patches.reshape(tokens, HEADS, HEAD_DIM), section * chunk_tokens, chunk_tokens, 0
    ).transpose(1, 0, 2)
    mine = lax.all_to_all(mine, OWNERS, 0, 0, tiled=True)
    fresh = [mine.reshape(sources * chunk_tokens, HEAD_DIM)]
    for c in range(1, CHUNKS):
        fresh.append(lax.ppermute(fresh[0], "section", [(c, 0)]))
    tables = []
    for which in range(2):
        moved = lax.all_to_all(by_head[which], OWNERS, 0, 0, tiled=True)
        tables.append(spread(moved.reshape(sources * tokens, HEAD_DIM)))
    k_parts, v_parts = tables

    query_blocks = patch_rows // QUERY_BLOCK
    lists = lax.dynamic_index_in_dim(block_lists[0], owner, 0, keepdims=False)
    lists = lists.reshape(micro_count, sources, 2, 2, query_blocks, SLOTS)
    lists = lax.dynamic_slice(
        lists, (0, 0, yl, core, 0, 0), (micro_count, sources, 1, 1, query_blocks, SLOTS)
    )
    lists = lists.reshape(micro_count, sources, query_blocks, SLOTS).transpose(0, 2, 1, 3)
    lists = lists.reshape(CHUNKS, -1, sources, SLOTS).transpose(0, 2, 1, 3)
    per_shard = patch_rows // KEY_BLOCK
    per_micro = per_shard * sources * 4
    micro, rest = lists // per_micro, lists % per_micro
    shard, half = rest // per_shard, rest % per_shard
    piece = ((shard % 2) ^ core) * 2 + ((shard // 2 % 2) ^ yl)
    places = ((piece * sources + shard // 4) * micro_count + micro) * patch_rows + half * KEY_BLOCK
    places = places.reshape(-1)
    chunk_entries = places.shape[0] // CHUNKS
    count = lax.dynamic_index_in_dim(block_counts[0], owner, 0, keepdims=False)
    gain = lax.dynamic_index_in_dim(query_gain.reshape(HEADS, HEAD_DIM), owner, 0)
    gate = lax.dynamic_index_in_dim(branch_gate.reshape(HEADS, HEAD_DIM), owner, 0)

    steps = CHUNKS + SECTIONS - 1
    results = []
    received = None
    for step in range(steps):
        if step == 0:
            x = fresh[0]
        elif step < CHUNKS:
            x = jnp.where(section == 0, fresh[step], received)
        else:
            x = received
        chunk = step - section
        active = ((chunk >= 0) & (chunk < CHUNKS)).astype(jnp.int32)
        meta = jnp.stack([active, jnp.clip(chunk, 0, CHUNKS - 1) * chunk_entries, count])
        result = attend(places, meta, x, gain, gate, k_parts, v_parts)
        results.append(result)
        if step < steps - 1:
            received = lax.ppermute(
                result, "section", [(s, s + 1) for s in range(SECTIONS - 1)]
            )
    done = lax.dynamic_slice_in_dim(jnp.stack(results), section, CHUNKS, 0)
    done = done.reshape(CHUNKS, sources, chunk_tokens, HEAD_DIM).transpose(1, 0, 2, 3)
    done = lax.all_to_all(done, OWNERS, 0, 0, tiled=True)
    done = done.reshape(HEADS, micro_count, patch_rows, HEAD_DIM).transpose(1, 2, 0, 3)
    return done.reshape(1, micro_count, patch_rows, channels)


def solution(mesh):
    fine = Mesh(
        mesh.devices.reshape(SECTIONS, -1, 2, 2, 2), ("section", "z", "yh", "yl", "core")
    )
    seq = ("z", "yh", "yl", "core")
    return jax.shard_map(
        local,
        mesh=fine,
        in_specs=(
            P(None, seq, None),
            P("section", None, seq, None),
            P("section", None, None, None),
            P("section", None),
            P("section", None),
            P("section", None),
        ),
        out_specs=P("section", None, seq, None),
        check_vma=False,
    )
```

```python
import functools

import jax
import jax.numpy as jnp
from jax import lax
from jax.experimental import pallas as pl
from jax.experimental.pallas import tpu as pltpu
from jax.sharding import Mesh, PartitionSpec as P

HEADS = 16
HEAD_DIM = 128
QUERY_BLOCK = 16
KEY_BLOCK = 32
SLOTS = 16
SECTIONS = 4
CHUNKS = 4
DELAY = 2
EARLY = 2
GROUP = 8
SPAN = SLOTS * KEY_BLOCK
SCORE_FLOOR = -1e30

OWNERS = ("z", "yh")


def attend_kernel(
    places, meta, x_ref, gain_ref, gate_ref, *rest, pieces, groups
):
    k_parts = rest[:pieces]
    v_parts = rest[pieces : 2 * pieces]
    out_ref, k_tab, v_tab, sems = rest[2 * pieces :]
    rows = k_tab.shape[0] // pieces
    base = meta[1]
    live_keys = meta[2] * KEY_BLOCK

    @pl.when(meta[0] > 0)
    def _():
        copies = []
        for which, (parts, tab) in enumerate(((k_parts, k_tab), (v_parts, v_tab))):
            for p in range(pieces):
                copy = pltpu.make_async_copy(
                    parts[p], tab.at[pl.ds(p * rows, rows), :], sems.at[which, p]
                )
                copy.start()
                copies.append(copy)
        for copy in copies:
            copy.wait()

        def one_group(index, carry):
            row0 = pl.multiple_of(index * (GROUP * QUERY_BLOCK), GROUP * QUERY_BLOCK)
            wide = x_ref[pl.ds(row0, GROUP * QUERY_BLOCK), :].astype(jnp.float32)
            mean = jnp.mean(wide * wide, axis=-1, keepdims=True)
            queries = (wide * lax.rsqrt(mean + 1e-06) * gain_ref[...]).astype(jnp.bfloat16)
            first = base + index * (GROUP * SLOTS)
            scores = []
            starts = []
            for g in range(GROUP):
                at = [
                    pl.multiple_of(places[first + g * SLOTS + j], KEY_BLOCK)
                    for j in range(SLOTS)
                ]
                starts.append(at)
                keys = jnp.concatenate(
                    [k_tab[pl.ds(a, KEY_BLOCK), :] for a in at], axis=0
                )
                scores.append(
                    lax.dot_general(
                        queries[g * QUERY_BLOCK : (g + 1) * QUERY_BLOCK],
                        keys,
                        (((1,), (1,)), ((), ())),
                        preferred_element_type=jnp.float32,
                    )
                )
            scores = jnp.concatenate(scores, axis=0) * (HEAD_DIM**-0.5)
            lane = lax.broadcasted_iota(jnp.int32, scores.shape, 1)
            scores = jnp.where(lane < live_keys, scores, SCORE_FLOOR)
            highest = jnp.max(scores, axis=-1, keepdims=True)
            exponent = jnp.exp(scores - highest)
            total = jnp.sum(exponent, axis=-1, keepdims=True)
            weights = (exponent / total).astype(jnp.bfloat16)
            summed = []
            for g in range(GROUP):
                values = jnp.concatenate(
                    [v_tab[pl.ds(a, KEY_BLOCK), :] for a in starts[g]], axis=0
                )
                summed.append(
                    jnp.dot(
                        weights[g * QUERY_BLOCK : (g + 1) * QUERY_BLOCK],
                        values,
                        preferred_element_type=jnp.float32,
                    )
                )
            heads = jnp.concatenate(summed, axis=0).astype(jnp.bfloat16)
            updated = wide + gate_ref[...] * heads.astype(jnp.float32)
            out_ref[pl.ds(row0, GROUP * QUERY_BLOCK), :] = updated.astype(jnp.bfloat16)
            return carry

        lax.fori_loop(0, groups, one_group, 0)

    @pl.when(meta[0] <= 0)
    def _():
        out_ref[...] = jnp.zeros_like(out_ref)


def attend(places, meta, x, gain, gate, k_parts, v_parts):
    pieces = len(k_parts)
    rows = k_parts[0].shape[0]
    total = pieces * rows
    queries = x.shape[0]
    vmem = pl.BlockSpec(memory_space=pltpu.VMEM)
    smem = pl.BlockSpec(memory_space=pltpu.SMEM)
    hbm = pl.BlockSpec(memory_space=pl.ANY)
    return pl.pallas_call(
        functools.partial(
            attend_kernel, pieces=pieces, groups=queries // (GROUP * QUERY_BLOCK)
        ),
        out_shape=jax.ShapeDtypeStruct(x.shape, jnp.bfloat16),
        in_specs=[smem, smem, vmem, vmem, vmem] + [hbm] * (2 * pieces),
        out_specs=vmem,
        scratch_shapes=[
            pltpu.VMEM((total, HEAD_DIM), jnp.bfloat16),
            pltpu.VMEM((total, HEAD_DIM), jnp.bfloat16),
            pltpu.SemaphoreType.DMA((2, pieces)),
        ],
        compiler_params=pltpu.CompilerParams(vmem_limit_bytes=24 * 1024 * 1024),
        cost_estimate=pl.CostEstimate(
            flops=4 * queries * SPAN * HEAD_DIM,
            bytes_accessed=2 * total * HEAD_DIM * 2,
            transcendentals=queries * SPAN,
        ),
    )(places, meta, x, gain, gate, *k_parts, *v_parts)


def swapped(value, axis):
    return lax.ppermute(value, axis, [(0, 1), (1, 0)])


def spread(value):
    other = swapped(value, "yl")
    return [value, other, swapped(value, "core"), swapped(other, "core")]


def local(patches, stale_cache, block_lists, block_counts, query_gain, branch_gate):
    section = lax.axis_index("section")
    owner = lax.axis_index("z") * lax.axis_size("yh") + lax.axis_index("yh")
    yl, core = lax.axis_index("yl"), lax.axis_index("core")
    micro_count, patch_rows, channels = patches.shape
    sources = lax.axis_size("z") * lax.axis_size("yh")
    tokens = micro_count * patch_rows
    chunk_tokens = tokens // CHUNKS

    by_head = stale_cache[0].reshape(tokens, 2, HEADS, HEAD_DIM).transpose(1, 2, 0, 3)
    mine = lax.dynamic_slice_in_dim(
        patches.reshape(tokens, HEADS, HEAD_DIM), section * chunk_tokens, chunk_tokens, 0
    ).transpose(1, 0, 2)
    first = jnp.concatenate([by_head[0], mine], axis=1)
    first = lax.all_to_all(first, OWNERS, 0, 0, tiled=True)
    first, second = lax.optimization_barrier((first, by_head[1]))
    k_parts = spread(first[:, :tokens].reshape(sources * tokens, HEAD_DIM))
    fresh = [first[:, tokens:].reshape(sources * chunk_tokens, HEAD_DIM)]
    for c in range(1, CHUNKS):
        fresh.append(lax.ppermute(fresh[0], "section", [(c, 0)]))
    second = lax.all_to_all(second, OWNERS, 0, 0, tiled=True)
    v_parts = spread(second.reshape(sources * tokens, HEAD_DIM))

    query_blocks = patch_rows // QUERY_BLOCK
    lists = lax.dynamic_index_in_dim(block_lists[0], owner, 0, keepdims=False)
    lists = lists.reshape(micro_count, sources, 2, 2, query_blocks, SLOTS)
    lists = lax.dynamic_slice(
        lists, (0, 0, yl, core, 0, 0), (micro_count, sources, 1, 1, query_blocks, SLOTS)
    )
    lists = lists.reshape(micro_count, sources, query_blocks, SLOTS).transpose(0, 2, 1, 3)
    lists = lists.reshape(CHUNKS, -1, sources, SLOTS).transpose(0, 2, 1, 3)
    per_shard = patch_rows // KEY_BLOCK
    per_micro = per_shard * sources * 4
    micro, rest = lists // per_micro, lists % per_micro
    shard, half = rest // per_shard, rest % per_shard
    piece = ((shard % 2) ^ core) * 2 + ((shard // 2 % 2) ^ yl)
    places = ((piece * sources + shard // 4) * micro_count + micro) * patch_rows + half * KEY_BLOCK
    places = places.reshape(-1)
    chunk_entries = places.shape[0] // CHUNKS
    count = lax.dynamic_index_in_dim(block_counts[0], owner, 0, keepdims=False)
    gain = lax.dynamic_index_in_dim(query_gain.reshape(HEADS, HEAD_DIM), owner, 0)
    gate = lax.dynamic_index_in_dim(branch_gate.reshape(HEADS, HEAD_DIM), owner, 0)

    def collected(chunks):
        done = []
        for c in chunks:
            own = results[c]
            for s in range(1, SECTIONS):
                own = jnp.where(section == s, results[c + s * DELAY], own)
            done.append(own.reshape(sources, chunk_tokens, HEAD_DIM))
        return jnp.concatenate(done, axis=1)

    steps = CHUNKS + (SECTIONS - 1) * DELAY
    results = []
    sent = []
    for step in range(steps):
        if step < DELAY:
            x = fresh[step]
        elif step < CHUNKS:
            x = jnp.where(section == 0, fresh[step], sent[step - DELAY])
        else:
            x = sent[step - DELAY]
        if step > 0:
            x, results[-1] = lax.optimization_barrier((x, results[-1]))
        chunk = step - section * DELAY
        active = ((chunk >= 0) & (chunk < CHUNKS)).astype(jnp.int32)
        meta = jnp.stack([active, jnp.clip(chunk, 0, CHUNKS - 1) * chunk_entries, count])
        results.append(attend(places, meta, x, gain, gate, k_parts, v_parts))
        if step + DELAY < steps:
            sent.append(
                lax.ppermute(
                    results[-1], "section", [(s, s + 1) for s in range(SECTIONS - 1)]
                )
            )
        if step == EARLY - 1 + (SECTIONS - 1) * DELAY:
            early = collected(range(EARLY))
            early, results[-1] = lax.optimization_barrier((early, results[-1]))
            early = lax.all_to_all(early, OWNERS, 0, 0, tiled=True)
    late = collected(range(EARLY, CHUNKS))
    late, early = lax.optimization_barrier((late, early))
    late = lax.all_to_all(late, OWNERS, 0, 0, tiled=True)
    done = jnp.concatenate([early, late], axis=1)
    done = done.reshape(HEADS, micro_count, patch_rows, HEAD_DIM).transpose(1, 2, 0, 3)
    return done.reshape(1, micro_count, patch_rows, channels)


def solution(mesh):
    fine = Mesh(
        mesh.devices.reshape(SECTIONS, -1, 2, 2, 2), ("section", "z", "yh", "yl", "core")
    )
    seq = ("z", "yh", "yl", "core")
    return jax.shard_map(
        local,
        mesh=fine,
        in_specs=(
            P(None, seq, None),
            P("section", None, seq, None),
            P("section", None, None, None),
            P("section", None),
            P("section", None),
            P("section", None),
        ),
        out_specs=P("section", None, seq, None),
        check_vma=False,
    )
```

```python
import functools

import jax
import jax.numpy as jnp
from jax import lax
from jax.experimental import pallas as pl
from jax.experimental.pallas import tpu as pltpu
from jax.sharding import Mesh, PartitionSpec as P

HEADS = 16
HEAD_DIM = 128
QUERY_BLOCK = 16
KEY_BLOCK = 32
SLOTS = 16
SECTIONS = 4
CHUNKS = 4
DELAY = 2
GROUP = 16
SPAN = SLOTS * KEY_BLOCK
SCORE_FLOOR = -1e30

OWNERS = ("z", "yh")


def gather_kernel(*refs, pieces):
    tables = refs[2 * pieces : 2 * pieces + 2]
    sems = refs[-1]
    copies = []
    for which in range(2):
        for p in range(pieces):
            part = refs[which * pieces + p]
            sources, tokens = part.shape[:2]
            copies.append(
                pltpu.make_async_copy(
                    part, tables[which].at[pl.ds(p * sources, sources)], sems.at[which, p]
                )
            )
    for copy in copies:
        copy.start()
    for copy in copies:
        copy.wait()


def gathered(k_parts, v_parts):
    pieces = len(k_parts)
    sources, tokens, width = k_parts[0].shape
    table = jax.ShapeDtypeStruct((pieces * sources, tokens, width), jnp.bfloat16)
    vmem = pl.BlockSpec(memory_space=pltpu.VMEM)
    k_tab, v_tab = pl.pallas_call(
        functools.partial(gather_kernel, pieces=pieces),
        out_shape=(table, table),
        in_specs=[pl.BlockSpec(memory_space=pl.ANY)] * (2 * pieces),
        out_specs=(vmem, vmem),
        scratch_shapes=[pltpu.SemaphoreType.DMA((2, pieces))],
        compiler_params=pltpu.CompilerParams(vmem_limit_bytes=24 * 1024 * 1024),
    )(*k_parts, *v_parts)
    rows = pieces * sources * tokens
    return k_tab.reshape(rows, width), v_tab.reshape(rows, width)


def attend_kernel(places, info, *rest, step, fresh, received):
    refs = list(rest)
    fresh_ref = refs.pop(0) if fresh else None
    received_ref = refs.pop(0) if received else None
    gain_ref, gate_ref, k_tab, v_tab = refs[:4]
    out_ref, done_ref = refs[-2:]
    section = info[0]
    chunk = step - section * DELAY
    live_keys = info[1] * KEY_BLOCK
    rows = out_ref.shape[0]
    chunk_tokens = done_ref.shape[1] // CHUNKS
    group_rows = GROUP * QUERY_BLOCK
    group_sources = group_rows // chunk_tokens

    @pl.when((chunk >= 0) & (chunk < CHUNKS))
    def _():
        base = chunk * (rows // QUERY_BLOCK * SLOTS)
        token0 = pl.multiple_of(chunk * chunk_tokens, chunk_tokens)

        def one_group(index, carry):
            row0 = pl.multiple_of(index * group_rows, group_rows)
            here = pl.ds(row0, group_rows)
            if fresh and received:
                x = jnp.where(section == 0, fresh_ref[here, :], received_ref[here, :])
            else:
                x = (fresh_ref if fresh else received_ref)[here, :]
            wide = x.astype(jnp.float32)
            mean = jnp.mean(wide * wide, axis=-1, keepdims=True)
            queries = (wide * lax.rsqrt(mean + 1e-06) * gain_ref[...]).astype(jnp.bfloat16)
            first = base + index * (GROUP * SLOTS)
            scores = []
            starts = []
            for g in range(GROUP):
                at = [
                    pl.multiple_of(places[first + g * SLOTS + j], KEY_BLOCK)
                    for j in range(SLOTS)
                ]
                starts.append(at)
                keys = jnp.concatenate(
                    [k_tab[pl.ds(a, KEY_BLOCK), :] for a in at], axis=0
                )
                scores.append(
                    lax.dot_general(
                        queries[g * QUERY_BLOCK : (g + 1) * QUERY_BLOCK],
                        keys,
                        (((1,), (1,)), ((), ())),
                        preferred_element_type=jnp.float32,
                    )
                )
            scores = jnp.concatenate(scores, axis=0) * (HEAD_DIM**-0.5)
            lane = lax.broadcasted_iota(jnp.int32, scores.shape, 1)
            scores = jnp.where(lane < live_keys, scores, SCORE_FLOOR)
            highest = jnp.max(scores, axis=-1, keepdims=True)
            exponent = jnp.exp(scores - highest)
            total = jnp.sum(exponent, axis=-1, keepdims=True)
            weights = (exponent / total).astype(jnp.bfloat16)
            summed = []
            for g in range(GROUP):
                values = jnp.concatenate(
                    [v_tab[pl.ds(a, KEY_BLOCK), :] for a in starts[g]], axis=0
                )
                summed.append(
                    jnp.dot(
                        weights[g * QUERY_BLOCK : (g + 1) * QUERY_BLOCK],
                        values,
                        preferred_element_type=jnp.float32,
                    )
                )
            heads = jnp.concatenate(summed, axis=0).astype(jnp.bfloat16)
            updated = wide + gate_ref[...] * heads.astype(jnp.float32)
            updated = updated.astype(jnp.bfloat16)
            out_ref[here, :] = updated
            done_ref[pl.ds(index * group_sources, group_sources), pl.ds(token0, chunk_tokens), :] = (
                updated.reshape(group_sources, chunk_tokens, HEAD_DIM)
            )
            return carry

        lax.fori_loop(0, rows // group_rows, one_group, 0)


def attend(step, places, info, fresh, received, gain, gate, k_tab, v_tab, done):
    inputs = [value for value in (fresh, received) if value is not None]
    rows, width = inputs[0].shape
    vmem = pl.BlockSpec(memory_space=pltpu.VMEM)
    smem = pl.BlockSpec(memory_space=pltpu.SMEM)
    inputs = [places, info, *inputs, gain, gate, k_tab, v_tab]
    aliases = {}
    done_shape = (CHUNKS * rows // HEADS // 8, HEADS * 8, width)
    if done is not None:
        aliases = {len(inputs): 1}
        inputs.append(done)
        done_shape = done.shape
    return pl.pallas_call(
        functools.partial(
            attend_kernel,
            step=step,
            fresh=fresh is not None,
            received=received is not None,
        ),
        out_shape=(
            jax.ShapeDtypeStruct((rows, width), jnp.bfloat16),
            jax.ShapeDtypeStruct(done_shape, jnp.bfloat16),
        ),
        in_specs=[smem, smem] + [vmem] * (len(inputs) - 2),
        out_specs=(vmem, vmem),
        input_output_aliases=aliases,
        compiler_params=pltpu.CompilerParams(vmem_limit_bytes=24 * 1024 * 1024),
        cost_estimate=pl.CostEstimate(
            flops=4 * rows * SPAN * HEAD_DIM,
            bytes_accessed=4 * rows * width,
            transcendentals=rows * SPAN,
        ),
    )(*inputs)


def swapped(value, axis):
    return lax.ppermute(value, axis, [(0, 1), (1, 0)])


def local(patches, stale_cache, block_lists, block_counts, query_gain, branch_gate):
    section = lax.axis_index("section")
    owner = lax.axis_index("z") * lax.axis_size("yh") + lax.axis_index("yh")
    yl, core = lax.axis_index("yl"), lax.axis_index("core")
    micro_count, patch_rows, channels = patches.shape
    sources = lax.axis_size("z") * lax.axis_size("yh")
    tokens = micro_count * patch_rows
    chunk_tokens = tokens // CHUNKS

    by_head = stale_cache[0].reshape(tokens, 2, HEADS, HEAD_DIM).transpose(2, 1, 0, 3)
    by_head = by_head.reshape(HEADS, 2 * tokens, HEAD_DIM)
    mine = lax.dynamic_slice_in_dim(
        patches.reshape(tokens, HEADS, HEAD_DIM), section * chunk_tokens, chunk_tokens, 0
    ).transpose(1, 0, 2)
    moved = lax.all_to_all(
        jnp.concatenate([by_head, mine], axis=1), OWNERS, 0, 0, tiled=True
    )
    k_own, v_own = moved[:, :tokens], moved[:, tokens : 2 * tokens]
    fresh = [moved[:, 2 * tokens :].reshape(sources * chunk_tokens, HEAD_DIM)]
    k_other = swapped(k_own, "yl")
    v_other = swapped(v_own, "yl")
    for c in range(1, CHUNKS):
        fresh.append(lax.ppermute(fresh[0], "section", [(c, 0)]))

    query_blocks = patch_rows // QUERY_BLOCK
    lists = lax.dynamic_index_in_dim(block_lists[0], owner, 0, keepdims=False)
    lists = lists.reshape(micro_count, sources, 2, 2, query_blocks, SLOTS)
    lists = lax.dynamic_slice(
        lists, (0, 0, yl, core, 0, 0), (micro_count, sources, 1, 1, query_blocks, SLOTS)
    )
    lists = lists.reshape(micro_count, sources, query_blocks, SLOTS).transpose(0, 2, 1, 3)
    lists = lists.reshape(CHUNKS, -1, sources, SLOTS).transpose(0, 2, 1, 3)
    per_shard = patch_rows // KEY_BLOCK
    per_micro = per_shard * sources * 4
    micro, rest = lists // per_micro, lists % per_micro
    shard, half = rest // per_shard, rest % per_shard
    piece = ((shard % 2) ^ core) * 2 + ((shard // 2 % 2) ^ yl)
    places = ((piece * sources + shard // 4) * micro_count + micro) * patch_rows + half * KEY_BLOCK
    places = places.reshape(-1)
    count = lax.dynamic_index_in_dim(block_counts[0], owner, 0, keepdims=False)
    info = jnp.stack([section, count]).astype(jnp.int32)
    gain = lax.dynamic_index_in_dim(query_gain.reshape(HEADS, HEAD_DIM), owner, 0)
    gate = lax.dynamic_index_in_dim(branch_gate.reshape(HEADS, HEAD_DIM), owner, 0)

    k_other, v_own, places, info, gain, gate, *fresh = lax.optimization_barrier(
        (k_other, v_own, places, info, gain, gate, *fresh)
    )
    k_parts = [k_own, k_other, swapped(k_own, "core"), swapped(k_other, "core")]
    v_parts = [v_own, v_other, swapped(v_own, "core"), swapped(v_other, "core")]
    k_tab, v_tab = gathered(k_parts, v_parts)

    steps = CHUNKS + (SECTIONS - 1) * DELAY
    sent = []
    result = done = None
    for step in range(steps):
        x = fresh[step] if step < CHUNKS else None
        received = sent[step - DELAY] if step >= DELAY else None
        result, done = attend(
            step, places, info, x, received, gain, gate, k_tab, v_tab, done
        )
        if step + DELAY < steps:
            sent.append(
                lax.ppermute(result, "section", [(s, s + 1) for s in range(SECTIONS - 1)])
            )
    done = lax.all_to_all(done, OWNERS, 0, 0, tiled=True)
    done = done.reshape(HEADS, micro_count, patch_rows, HEAD_DIM).transpose(1, 2, 0, 3)
    return done.reshape(1, micro_count, patch_rows, channels)


def solution(mesh):
    fine = Mesh(
        mesh.devices.reshape(SECTIONS, -1, 2, 2, 2), ("section", "z", "yh", "yl", "core")
    )
    seq = ("z", "yh", "yl", "core")
    return jax.shard_map(
        local,
        mesh=fine,
        in_specs=(
            P(None, seq, None),
            P("section", None, seq, None),
            P("section", None, None, None),
            P("section", None),
            P("section", None),
            P("section", None),
        ),
        out_specs=P("section", None, seq, None),
        check_vma=False,
    )
```

```python
import functools

import jax
import jax.numpy as jnp
from jax import lax
from jax.experimental import pallas as pl
from jax.experimental.pallas import tpu as pltpu
from jax.sharding import PartitionSpec as P

HEADS = 16
HEAD_DIM = 128
QUERY_BLOCK = 16
KEY_BLOCK = 32
SLOTS = 16
SECTIONS = 4
CHUNKS = 4
DELAY = 2
GROUP = 32
SPAN = SLOTS * KEY_BLOCK
SCORE_FLOOR = -1e30

RINGS = 8
SHIFTS = (0, 1, -1, 2, -2, 3, -3, 4)
WAVES = ((0, 1, 2, 3), (4, 5, 6, 7))


def pack_kernel(cache, patches, *refs, shifts):
    outs, sems = refs[: len(shifts)], refs[-1]
    section, shard = lax.axis_index("section"), lax.axis_index("seq")
    z, upper = shard // RINGS, shard // 4 % 2
    micro_count, rows = cache.shape[:2]
    depth = len(shifts)
    channels = patches.shape[2]
    chunk_tokens = outs[0].shape[1] - 2 * micro_count * rows
    token0 = section * chunk_tokens
    fresh_rows = pl.ds(pl.multiple_of(token0 % rows, chunk_tokens), chunk_tokens)
    copies = []
    for k, shift in enumerate(shifts):
        for other in range(2):
            head = lax.rem(z + (shift + depth), depth) * 2 + (upper ^ other)
            slot = len(copies)
            for which in range(2):
                start = pl.multiple_of(which * channels + head * HEAD_DIM, HEAD_DIM)
                for m in range(micro_count):
                    copies.append(
                        pltpu.make_async_copy(
                            cache.at[m, :, pl.ds(start, HEAD_DIM)],
                            outs[k].at[other, pl.ds((which * micro_count + m) * rows, rows), :],
                            sems.at[slot + which * micro_count + m],
                        )
                    )
            start = pl.multiple_of(head * HEAD_DIM, HEAD_DIM)
            copies.append(
                pltpu.make_async_copy(
                    patches.at[token0 // rows, fresh_rows, pl.ds(start, HEAD_DIM)],
                    outs[k].at[other, pl.ds(2 * micro_count * rows, chunk_tokens), :],
                    sems.at[slot + 2 * micro_count],
                )
            )
    for copy in copies:
        copy.start()
    for copy in copies:
        copy.wait()


def packed(cache, patches):
    micro_count, rows, channels = patches.shape
    tokens = micro_count * rows
    piece = jax.ShapeDtypeStruct((2, 2 * tokens + tokens // CHUNKS, HEAD_DIM), jnp.bfloat16)
    count = len(SHIFTS)
    return pl.pallas_call(
        functools.partial(pack_kernel, shifts=SHIFTS),
        out_shape=(piece,) * count,
        in_specs=[pl.BlockSpec(memory_space=pltpu.HBM)] * 2,
        out_specs=(pl.BlockSpec(memory_space=pltpu.VMEM),) * count,
        scratch_shapes=[pltpu.SemaphoreType.DMA((count * 2 * (2 * micro_count + 1),))],
        compiler_params=pltpu.CompilerParams(vmem_limit_bytes=61 * 1024 * 1024),
    )(cache, patches)


def part_kernel(*refs, count):
    own, others, sems = refs[count], refs[count + 1 : -1], refs[-1]
    copies = []
    for wave, other in zip(WAVES, others):
        for n, k in enumerate(wave):
            copies.append(pltpu.make_async_copy(refs[k].at[1], other.at[n], sems.at[0, k]))
            copies.append(
                pltpu.make_async_copy(
                    refs[k].at[0, pl.ds(0, own.shape[1]), :], own.at[k], sems.at[1, k]
                )
            )
    for copy in copies:
        copy.start()
    for copy in copies:
        copy.wait()


def parted(pieces, rows):
    count = len(pieces)
    vmem = pl.BlockSpec(memory_space=pltpu.VMEM)
    own, *others = pl.pallas_call(
        functools.partial(part_kernel, count=count),
        out_shape=(
            jax.ShapeDtypeStruct((count, rows, HEAD_DIM), jnp.bfloat16),
            *(
                jax.ShapeDtypeStruct((len(wave), *pieces[0].shape[1:]), jnp.bfloat16)
                for wave in WAVES
            ),
        ),
        in_specs=[pl.BlockSpec(memory_space=pl.ANY)] * count,
        out_specs=(vmem,) * (1 + len(WAVES)),
        scratch_shapes=[pltpu.SemaphoreType.DMA((2, count))],
        compiler_params=pltpu.CompilerParams(vmem_limit_bytes=8 * 1024 * 1024),
    )(*pieces)
    return own, others


def arrange_kernel(info, *refs, skip):
    count = len(SHIFTS)
    pieces, crosses, out = refs[:count], refs[count:-1], refs[-1]
    z, upper = info[2], info[3]
    chunk_tokens = pieces[0].shape[1] - skip
    for wave, cross in zip(WAVES, crosses):
        for n, k in enumerate(wave):
            source = lax.rem(z + (count - SHIFTS[k]), count) * 2
            for part, index, lane in ((pieces[k], 0, upper), (cross, n, 1 - upper)):
                place = pl.multiple_of((source + lane) * chunk_tokens, chunk_tokens)
                out[pl.ds(place, chunk_tokens), :] = part[index, skip : skip + chunk_tokens, :]


def arranged(info, pieces, crosses, tokens, chunk_tokens):
    inputs = [*pieces, *crosses]
    rows = 2 * len(pieces) * chunk_tokens
    vmem = pl.BlockSpec(memory_space=pltpu.VMEM)
    return pl.pallas_call(
        functools.partial(arrange_kernel, skip=2 * tokens),
        out_shape=jax.ShapeDtypeStruct((rows, HEAD_DIM), jnp.bfloat16),
        in_specs=[pl.BlockSpec(memory_space=pltpu.SMEM)] + [vmem] * len(inputs),
        out_specs=vmem,
        compiler_params=pltpu.CompilerParams(vmem_limit_bytes=8 * 1024 * 1024),
    )(info, *inputs)


def gather_kernel(*refs, rows):
    parts, out, sems = refs[:-2], refs[-2], refs[-1]
    copies = []
    place = 0
    for n, part in enumerate(parts):
        size = part.shape[0]
        copies.append(
            pltpu.make_async_copy(
                part.at[:, pl.ds(0, rows), :], out.at[pl.ds(place, size)], sems.at[n]
            )
        )
        place += size
    for copy in copies:
        copy.start()
    for copy in copies:
        copy.wait()


def gathered(parts, rows):
    entries = sum(part.shape[0] for part in parts)
    return pl.pallas_call(
        functools.partial(gather_kernel, rows=rows),
        out_shape=jax.ShapeDtypeStruct((entries, rows, HEAD_DIM), jnp.bfloat16),
        in_specs=[pl.BlockSpec(memory_space=pl.ANY)] * len(parts),
        out_specs=pl.BlockSpec(memory_space=pltpu.VMEM),
        scratch_shapes=[pltpu.SemaphoreType.DMA((len(parts),))],
        compiler_params=pltpu.CompilerParams(vmem_limit_bytes=8 * 1024 * 1024),
    )(*parts)


def attend_kernel(places, info, *rest, step, fresh, received):
    refs = list(rest)
    fresh_ref = refs.pop(0) if fresh else None
    received_ref = refs.pop(0) if received else None
    gain_ref, gate_ref, table = refs[:3]
    out_ref, done_ref = refs[-2:]
    section = info[0]
    chunk = step - section * DELAY
    live_keys = info[1] * KEY_BLOCK
    rows = out_ref.shape[0]
    chunk_tokens = done_ref.shape[1] // CHUNKS
    group_rows = GROUP * QUERY_BLOCK
    value_rows = done_ref.shape[1]
    group_sources = group_rows // chunk_tokens

    @pl.when((chunk >= 0) & (chunk < CHUNKS))
    def _():
        base = chunk * (rows // QUERY_BLOCK * SLOTS)
        token0 = pl.multiple_of(chunk * chunk_tokens, chunk_tokens)

        def one_group(index, carry):
            row0 = pl.multiple_of(index * group_rows, group_rows)
            here = pl.ds(row0, group_rows)
            if fresh and received:
                x = jnp.where(section == 0, fresh_ref[here, :], received_ref[here, :])
            else:
                x = (fresh_ref if fresh else received_ref)[here, :]
            wide = x.astype(jnp.float32)
            mean = jnp.mean(wide * wide, axis=-1, keepdims=True)
            queries = (wide * lax.rsqrt(mean + 1e-06) * gain_ref[...]).astype(jnp.bfloat16)
            first = base + index * (GROUP * SLOTS)
            scores = []
            starts = []
            for g in range(GROUP):
                at = [
                    pl.multiple_of(places[first + g * SLOTS + j], KEY_BLOCK)
                    for j in range(SLOTS)
                ]
                starts.append(at)
                keys = jnp.concatenate(
                    [table[pl.ds(a, KEY_BLOCK), :] for a in at], axis=0
                )
                scores.append(
                    lax.dot_general(
                        queries[g * QUERY_BLOCK : (g + 1) * QUERY_BLOCK],
                        keys,
                        (((1,), (1,)), ((), ())),
                        preferred_element_type=jnp.float32,
                    )
                )
            scores = jnp.concatenate(scores, axis=0) * (HEAD_DIM**-0.5)
            lane = lax.broadcasted_iota(jnp.int32, scores.shape, 1)
            scores = jnp.where(lane < live_keys, scores, SCORE_FLOOR)
            highest = jnp.max(scores, axis=-1, keepdims=True)
            exponent = jnp.exp(scores - highest)
            total = jnp.sum(exponent, axis=-1, keepdims=True)
            weights = (exponent / total).astype(jnp.bfloat16)
            summed = []
            for g in range(GROUP):
                values = jnp.concatenate(
                    [table[pl.ds(a + value_rows, KEY_BLOCK), :] for a in starts[g]],
                    axis=0,
                )
                summed.append(
                    jnp.dot(
                        weights[g * QUERY_BLOCK : (g + 1) * QUERY_BLOCK],
                        values,
                        preferred_element_type=jnp.float32,
                    )
                )
            heads = jnp.concatenate(summed, axis=0).astype(jnp.bfloat16)
            updated = wide + gate_ref[...] * heads.astype(jnp.float32)
            updated = updated.astype(jnp.bfloat16)
            out_ref[here, :] = updated
            done_ref[pl.ds(index * group_sources, group_sources), pl.ds(token0, chunk_tokens), :] = (
                updated.reshape(group_sources, chunk_tokens, HEAD_DIM)
            )
            return carry

        lax.fori_loop(0, rows // group_rows, one_group, 0)


def attend(step, places, info, fresh, received, gain, gate, table, done):
    inputs = [value for value in (fresh, received) if value is not None]
    rows, width = inputs[0].shape
    vmem = pl.BlockSpec(memory_space=pltpu.VMEM)
    smem = pl.BlockSpec(memory_space=pltpu.SMEM)
    inputs = [places, info, *inputs, gain, gate, table]
    aliases = {}
    done_shape = (CHUNKS * rows // HEADS // 8, HEADS * 8, width)
    if done is not None:
        aliases = {len(inputs): 1}
        inputs.append(done)
        done_shape = done.shape
    return pl.pallas_call(
        functools.partial(
            attend_kernel,
            step=step,
            fresh=fresh is not None,
            received=received is not None,
        ),
        out_shape=(
            jax.ShapeDtypeStruct((rows, width), jnp.bfloat16),
            jax.ShapeDtypeStruct(done_shape, jnp.bfloat16),
        ),
        in_specs=[smem, smem] + [vmem] * (len(inputs) - 2),
        out_specs=(vmem, vmem),
        input_output_aliases=aliases,
        compiler_params=pltpu.CompilerParams(vmem_limit_bytes=8 * 1024 * 1024),
        cost_estimate=pl.CostEstimate(
            flops=4 * rows * SPAN * HEAD_DIM,
            bytes_accessed=4 * rows * width,
            transcendentals=rows * SPAN,
        ),
    )(*inputs)


def moved(value, rule):
    total = lax.axis_size("seq")
    pairs = []
    for place in range(total):
        z, y, core = place // RINGS, place // 2 % 4, place % 2
        z, y, core = rule(z, y, core)
        pairs.append((place, z % (total // RINGS) * RINGS + y * 2 + core))
    return lax.ppermute(value, "seq", pairs)


def across(value):
    return moved(value, lambda z, y, core: (z, 3 - y, core))


def beside(value):
    return moved(value, lambda z, y, core: (z, y ^ 1, core))


def twin(value):
    return moved(value, lambda z, y, core: (z, y, core ^ 1))


def local(patches, stale_cache, block_lists, block_counts, query_gain, branch_gate):
    section = lax.axis_index("section")
    shard = lax.axis_index("seq")
    depth = lax.axis_size("seq") // RINGS
    z, y, core = shard // RINGS, shard // 2 % 4, shard % 2
    upper = y // 2
    lane = jnp.minimum(y, 3 - y)
    owner = z * 2 + upper
    micro_count, patch_rows, channels = patches.shape
    sources = 2 * depth
    tokens = micro_count * patch_rows
    chunk_tokens = tokens // CHUNKS

    count = lax.dynamic_index_in_dim(block_counts[0], owner, 0, keepdims=False)
    info = jnp.stack([section, count, z, upper]).astype(jnp.int32)
    pieces = list(packed(stale_cache[0], patches))
    for k in range(1, len(SHIFTS)):
        shift = SHIFTS[k]
        pieces[k] = moved(pieces[k], lambda z, y, core: (z + shift, y, core))

    own, others = parted(pieces, 2 * tokens)
    own_beside = beside(own)
    crosses = [across(other) for other in others]
    cross = [value[:, : 2 * tokens] for value in crosses]
    parts = [own, own_beside, *cross, *(beside(value) for value in cross)]
    parts = parts + [twin(part) for part in parts]

    fresh = [arranged(info, pieces, crosses, tokens, chunk_tokens)]
    for c in range(1, CHUNKS):
        fresh.append(lax.ppermute(fresh[0], "section", [(c, 0)]))

    query_blocks = patch_rows // QUERY_BLOCK
    lists = lax.dynamic_index_in_dim(block_lists[0], owner, 0, keepdims=False)
    lists = lists.reshape(micro_count, depth, 4, 2, query_blocks, SLOTS)
    lists = lax.dynamic_index_in_dim(lists, core, 3, keepdims=False)
    lists = jnp.stack(
        [
            lax.dynamic_index_in_dim(lists, lane, 2, keepdims=False),
            lax.dynamic_index_in_dim(lists, 3 - lane, 2, keepdims=False),
        ],
        axis=2,
    )
    lists = lists.reshape(micro_count, sources, query_blocks, SLOTS).transpose(0, 2, 1, 3)
    lists = lists.reshape(CHUNKS, -1, sources, SLOTS).transpose(0, 2, 1, 3)
    per_shard = patch_rows // KEY_BLOCK
    per_micro = per_shard * depth * RINGS
    micro, rest = lists // per_micro, lists % per_micro
    holder, half = rest // per_shard, rest % per_shard
    back = (z + depth - holder // RINGS) % depth
    slot = jnp.where(back <= depth // 2, jnp.maximum(2 * back - 1, 0), 2 * (depth - back))
    row = holder // 2 % 4
    side = jnp.where(
        row == y, 0, jnp.where(row == (y ^ 1), 1, jnp.where(row == 3 - y, 2, 3))
    )
    entry = ((holder % 2 ^ core) * 4 + side) * depth + slot
    places = (entry * 2 * micro_count + micro) * patch_rows + half * KEY_BLOCK
    places = places.reshape(-1)
    gain = lax.dynamic_index_in_dim(query_gain.reshape(HEADS, HEAD_DIM), owner, 0)
    gate = lax.dynamic_index_in_dim(branch_gate.reshape(HEADS, HEAD_DIM), owner, 0)

    table = gathered(parts, 2 * tokens)
    table = table.reshape(-1, HEAD_DIM)

    steps = CHUNKS + (SECTIONS - 1) * DELAY
    sent = []
    result = done = None
    for step in range(steps):
        x = fresh[step] if step < CHUNKS else None
        received = sent[step - DELAY] if step >= DELAY else None
        result, done = attend(
            step, places, info, x, received, gain, gate, table, done
        )
        if step + DELAY < steps:
            sent.append(
                lax.ppermute(result, "section", [(s, s + 1) for s in range(SECTIONS - 1)])
            )
    groups = [
        [place * RINGS + row * 2 + c for place in range(depth) for row in (first, 3 - first)]
        for first in range(2)
        for c in range(2)
    ]
    done = lax.all_to_all(done, "seq", 0, 0, axis_index_groups=groups, tiled=True)
    done = done.reshape(HEADS, micro_count, patch_rows, HEAD_DIM).transpose(1, 2, 0, 3)
    return done.reshape(1, micro_count, patch_rows, channels)


def solution(mesh):
    return jax.shard_map(
        local,
        mesh=mesh,
        in_specs=(
            P(None, "seq", None),
            P("section", None, "seq", None),
            P("section", None, None, None),
            P("section", None),
            P("section", None),
            P("section", None),
        ),
        out_specs=P("section", None, "seq", None),
        check_vma=False,
    )
```

```python
import functools

import jax
import jax.numpy as jnp
from jax import lax
from jax.experimental import pallas as pl
from jax.experimental.pallas import tpu as pltpu
from jax.sharding import PartitionSpec as P

HEADS = 16
HEAD_DIM = 128
QUERY_BLOCK = 16
KEY_BLOCK = 32
SLOTS = 16
SECTIONS = 4
CHUNKS = 4
DELAY = 2
GROUP = 32
SPAN = SLOTS * KEY_BLOCK
SCORE_FLOOR = -1e30

RINGS = 8
SHIFTS = (0, 1, -1, 2, -2, 3, -3, 4)
FIRST, REST = (1, 2, 3, 4), (0, 5, 6, 7)
WAVES = ((0, 1, 2, 3), (4, 5, 6, 7))


def pack_kernel(cache, patches, *refs, shifts):
    outs, sems = refs[: len(shifts)], refs[-1]
    section, shard = lax.axis_index("section"), lax.axis_index("seq")
    z, upper = shard // RINGS, shard // 4 % 2
    tokens, channels = patches.shape
    chunk_tokens = outs[0].shape[1] - 2 * tokens
    token0 = pl.multiple_of((section ^ (section // 2)) * chunk_tokens, chunk_tokens)
    copies = []
    for k, shift in enumerate(shifts):
        for other in range(2):
            head = lax.rem(z + (shift + len(SHIFTS)), len(SHIFTS)) * 2 + (upper ^ other)
            key0 = pl.multiple_of(head * HEAD_DIM, HEAD_DIM)
            value0 = pl.multiple_of(channels + head * HEAD_DIM, HEAD_DIM)
            for which, (source, place, size) in enumerate(
                (
                    (cache.at[:, pl.ds(key0, HEAD_DIM)], 0, tokens),
                    (cache.at[:, pl.ds(value0, HEAD_DIM)], tokens, tokens),
                    (
                        patches.at[pl.ds(token0, chunk_tokens), pl.ds(key0, HEAD_DIM)],
                        2 * tokens,
                        chunk_tokens,
                    ),
                )
            ):
                copies.append(
                    pltpu.make_async_copy(
                        source, outs[k].at[other, pl.ds(place, size), :], sems.at[len(copies)]
                    )
                )
    for copy in copies:
        copy.start()
    for copy in copies:
        copy.wait()


def packed(cache, patches, shifts):
    tokens = patches.shape[0]
    piece = jax.ShapeDtypeStruct((2, 2 * tokens + tokens // CHUNKS, HEAD_DIM), jnp.bfloat16)
    count = len(shifts)
    return pl.pallas_call(
        functools.partial(pack_kernel, shifts=shifts),
        out_shape=(piece,) * count,
        in_specs=[pl.BlockSpec(memory_space=pltpu.HBM)] * 2,
        out_specs=(pl.BlockSpec(memory_space=pltpu.VMEM),) * count,
        scratch_shapes=[pltpu.SemaphoreType.DMA((count * 6,))],
        compiler_params=pltpu.CompilerParams(vmem_limit_bytes=61 * 1024 * 1024),
    )(cache, patches)


def part_kernel(*refs, count):
    own, others, sems = refs[count], refs[count + 1 : -1], refs[-1]
    copies = []
    for wave, other in zip(WAVES, others):
        for n, k in enumerate(wave):
            copies.append(pltpu.make_async_copy(refs[k].at[1], other.at[n], sems.at[0, k]))
            copies.append(
                pltpu.make_async_copy(
                    refs[k].at[0, pl.ds(0, own.shape[1]), :], own.at[k], sems.at[1, k]
                )
            )
    for copy in copies:
        copy.start()
    for copy in copies:
        copy.wait()


def parted(pieces, rows):
    count = len(pieces)
    own, *others = pl.pallas_call(
        functools.partial(part_kernel, count=count),
        out_shape=(
            jax.ShapeDtypeStruct((count, rows, HEAD_DIM), jnp.bfloat16),
            *(
                jax.ShapeDtypeStruct((len(wave), *pieces[0].shape[1:]), jnp.bfloat16)
                for wave in WAVES
            ),
        ),
        in_specs=[pl.BlockSpec(memory_space=pl.ANY)] * count,
        out_specs=(pl.BlockSpec(memory_space=pl.ANY),) * (1 + len(WAVES)),
        scratch_shapes=[pltpu.SemaphoreType.DMA((2, count))],
        compiler_params=pltpu.CompilerParams(vmem_limit_bytes=8 * 1024 * 1024),
    )(*pieces)
    return own, others


def arrange_kernel(info, *refs, skip):
    count = len(SHIFTS)
    pieces, crosses, out = refs[:count], refs[count:-1], refs[-1]
    z, upper = info[2], info[3]
    chunk_tokens = pieces[0].shape[1] - skip
    for wave, cross in zip(WAVES, crosses):
        for n, k in enumerate(wave):
            source = lax.rem(z + (count - SHIFTS[k]), count) * 2
            for part, index, lane in ((pieces[k], 0, upper), (cross, n, 1 - upper)):
                place = pl.multiple_of((source + lane) * chunk_tokens, chunk_tokens)
                out[pl.ds(place, chunk_tokens), :] = part[index, skip : skip + chunk_tokens, :]


def arranged(info, pieces, crosses, tokens, chunk_tokens):
    inputs = [*pieces, *crosses]
    rows = 2 * len(pieces) * chunk_tokens
    vmem = pl.BlockSpec(memory_space=pltpu.VMEM)
    return pl.pallas_call(
        functools.partial(arrange_kernel, skip=2 * tokens),
        out_shape=jax.ShapeDtypeStruct((rows, HEAD_DIM), jnp.bfloat16),
        in_specs=[pl.BlockSpec(memory_space=pltpu.SMEM)] + [vmem] * len(inputs),
        out_specs=vmem,
        compiler_params=pltpu.CompilerParams(vmem_limit_bytes=8 * 1024 * 1024),
    )(info, *inputs)


def gather_kernel(*refs, rows):
    parts, out, sems = refs[:-2], refs[-2], refs[-1]
    copies = []
    place = 0
    for n, part in enumerate(parts):
        size = part.shape[0]
        copies.append(
            pltpu.make_async_copy(
                part.at[:, pl.ds(0, rows), :], out.at[pl.ds(place, size)], sems.at[n]
            )
        )
        place += size
    for copy in copies:
        copy.start()
    for copy in copies:
        copy.wait()


def gathered(parts, rows):
    entries = sum(part.shape[0] for part in parts)
    return pl.pallas_call(
        functools.partial(gather_kernel, rows=rows),
        out_shape=jax.ShapeDtypeStruct((entries, rows, HEAD_DIM), jnp.bfloat16),
        in_specs=[pl.BlockSpec(memory_space=pl.ANY)] * len(parts),
        out_specs=pl.BlockSpec(memory_space=pltpu.VMEM),
        scratch_shapes=[pltpu.SemaphoreType.DMA((len(parts),))],
        compiler_params=pltpu.CompilerParams(vmem_limit_bytes=8 * 1024 * 1024),
    )(*parts)


def attend_kernel(places, info, x_ref, *refs, step):
    gain_ref, gate_ref, table = refs[:3]
    out_ref, done_ref = refs[-2:]
    section = info[0]
    chunk = step - section * DELAY
    live_keys = info[1] * KEY_BLOCK
    rows = out_ref.shape[0]
    chunk_tokens = done_ref.shape[1] // CHUNKS
    group_rows = GROUP * QUERY_BLOCK
    value_rows = done_ref.shape[1]
    group_sources = group_rows // chunk_tokens

    @pl.when((chunk >= 0) & (chunk < CHUNKS))
    def _():
        base = chunk * (rows // QUERY_BLOCK * SLOTS)
        token0 = pl.multiple_of(chunk * chunk_tokens, chunk_tokens)

        def one_group(index, carry):
            row0 = pl.multiple_of(index * group_rows, group_rows)
            here = pl.ds(row0, group_rows)
            wide = x_ref[here, :].astype(jnp.float32)
            mean = jnp.mean(wide * wide, axis=-1, keepdims=True)
            queries = (wide * lax.rsqrt(mean + 1e-06) * gain_ref[...]).astype(jnp.bfloat16)
            first = base + index * (GROUP * SLOTS)
            scores = []
            starts = []
            for g in range(GROUP):
                at = [
                    pl.multiple_of(places[first + g * SLOTS + j], KEY_BLOCK)
                    for j in range(SLOTS)
                ]
                starts.append(at)
                keys = jnp.concatenate(
                    [table[pl.ds(a, KEY_BLOCK), :] for a in at], axis=0
                )
                scores.append(
                    lax.dot_general(
                        queries[g * QUERY_BLOCK : (g + 1) * QUERY_BLOCK],
                        keys,
                        (((1,), (1,)), ((), ())),
                        preferred_element_type=jnp.float32,
                    )
                )
            scores = jnp.concatenate(scores, axis=0) * (HEAD_DIM**-0.5)
            lane = lax.broadcasted_iota(jnp.int32, scores.shape, 1)
            scores = jnp.where(lane < live_keys, scores, SCORE_FLOOR)
            highest = jnp.max(scores, axis=-1, keepdims=True)
            exponent = jnp.exp(scores - highest)
            total = jnp.sum(exponent, axis=-1, keepdims=True)
            weights = (exponent / total).astype(jnp.bfloat16)
            summed = []
            for g in range(GROUP):
                values = jnp.concatenate(
                    [table[pl.ds(a + value_rows, KEY_BLOCK), :] for a in starts[g]],
                    axis=0,
                )
                summed.append(
                    jnp.dot(
                        weights[g * QUERY_BLOCK : (g + 1) * QUERY_BLOCK],
                        values,
                        preferred_element_type=jnp.float32,
                    )
                )
            heads = jnp.concatenate(summed, axis=0).astype(jnp.bfloat16)
            updated = wide + gate_ref[...] * heads.astype(jnp.float32)
            updated = updated.astype(jnp.bfloat16)
            out_ref[here, :] = updated
            done_ref[pl.ds(index * group_sources, group_sources), pl.ds(token0, chunk_tokens), :] = (
                updated.reshape(group_sources, chunk_tokens, HEAD_DIM)
            )
            return carry

        lax.fori_loop(0, rows // group_rows, one_group, 0)

    if step < DELAY:

        @pl.when(section == SECTIONS - 1)
        def _():
            out_ref[...] = x_ref[...]


def attend(step, places, info, x, gain, gate, table, done):
    rows, width = x.shape
    vmem = pl.BlockSpec(memory_space=pltpu.VMEM)
    smem = pl.BlockSpec(memory_space=pltpu.SMEM)
    inputs = [places, info, x, gain, gate, table]
    aliases = {}
    done_shape = (CHUNKS * rows // HEADS // 8, HEADS * 8, width)
    if done is not None:
        aliases = {len(inputs): 1}
        inputs.append(done)
        done_shape = done.shape
    return pl.pallas_call(
        functools.partial(attend_kernel, step=step),
        out_shape=(
            jax.ShapeDtypeStruct((rows, width), jnp.bfloat16),
            jax.ShapeDtypeStruct(done_shape, jnp.bfloat16),
        ),
        in_specs=[smem, smem] + [vmem] * (len(inputs) - 2),
        out_specs=(vmem, vmem),
        input_output_aliases=aliases,
        compiler_params=pltpu.CompilerParams(vmem_limit_bytes=8 * 1024 * 1024),
        cost_estimate=pl.CostEstimate(
            flops=4 * rows * SPAN * HEAD_DIM,
            bytes_accessed=4 * rows * width,
            transcendentals=rows * SPAN,
        ),
    )(*inputs)


def moved(value, rule):
    total = lax.axis_size("seq")
    pairs = []
    for place in range(total):
        z, y, core = place // RINGS, place // 2 % 4, place % 2
        z, y, core = rule(z, y, core)
        pairs.append((place, z % (total // RINGS) * RINGS + y * 2 + core))
    return lax.ppermute(value, "seq", pairs)


def across(value):
    return moved(value, lambda z, y, core: (z, 3 - y, core))


def beside(value):
    return moved(value, lambda z, y, core: (z, y ^ 1, core))


def twin(value):
    return moved(value, lambda z, y, core: (z, y, core ^ 1))


def local(patches, stale_cache, block_lists, block_counts, query_gain, branch_gate):
    section = lax.axis_index("section")
    shard = lax.axis_index("seq")
    depth = lax.axis_size("seq") // RINGS
    z, y, core = shard // RINGS, shard // 2 % 4, shard % 2
    upper = y // 2
    lane = jnp.minimum(y, 3 - y)
    owner = z * 2 + upper
    micro_count, patch_rows, channels = patches.shape
    sources = 2 * depth
    tokens = micro_count * patch_rows
    chunk_tokens = tokens // CHUNKS

    count = lax.dynamic_index_in_dim(block_counts[0], owner, 0, keepdims=False)
    info = jnp.stack([section, count, z, upper]).astype(jnp.int32)
    rows_in = (stale_cache.reshape(tokens, 2 * channels), patches.reshape(tokens, channels))
    pieces = [None] * depth
    for part in FIRST, REST:
        for k, piece in zip(part, packed(*rows_in, tuple(SHIFTS[k] for k in part))):
            pieces[k] = piece
    for k in range(1, len(SHIFTS)):
        shift = SHIFTS[k]
        pieces[k] = moved(pieces[k], lambda z, y, core: (z + shift, y, core))

    own, others = parted(pieces, 2 * tokens)
    own_beside = beside(own)
    crosses = [across(other) for other in others]
    cross = [value[:, : 2 * tokens] for value in crosses]
    parts = [own, own_beside, *cross, *(beside(value) for value in cross)]
    parts = parts + [twin(part) for part in parts]

    fresh = [arranged(info, pieces, crosses, tokens, chunk_tokens)]
    fresh.append(lax.ppermute(fresh[0], "section", [(1, 0), (2, 3)]))

    query_blocks = patch_rows // QUERY_BLOCK
    lists = lax.dynamic_index_in_dim(block_lists[0], owner, 0, keepdims=False)
    lists = lists.reshape(micro_count, depth, 4, 2, query_blocks, SLOTS)
    lists = lax.dynamic_index_in_dim(lists, core, 3, keepdims=False)
    lists = jnp.stack(
        [
            lax.dynamic_index_in_dim(lists, lane, 2, keepdims=False),
            lax.dynamic_index_in_dim(lists, 3 - lane, 2, keepdims=False),
        ],
        axis=2,
    )
    lists = lists.reshape(micro_count, sources, query_blocks, SLOTS).transpose(0, 2, 1, 3)
    lists = lists.reshape(CHUNKS, -1, sources, SLOTS).transpose(0, 2, 1, 3)
    per_shard = patch_rows // KEY_BLOCK
    per_micro = per_shard * depth * RINGS
    micro, rest = lists // per_micro, lists % per_micro
    holder, half = rest // per_shard, rest % per_shard
    back = (z + depth - holder // RINGS) % depth
    slot = jnp.where(back <= depth // 2, jnp.maximum(2 * back - 1, 0), 2 * (depth - back))
    row = holder // 2 % 4
    side = jnp.where(
        row == y, 0, jnp.where(row == (y ^ 1), 1, jnp.where(row == 3 - y, 2, 3))
    )
    entry = ((holder % 2 ^ core) * 4 + side) * depth + slot
    places = (entry * 2 * micro_count + micro) * patch_rows + half * KEY_BLOCK
    places = places.reshape(-1)
    gain = lax.dynamic_index_in_dim(query_gain.reshape(HEADS, HEAD_DIM), owner, 0)
    gate = lax.dynamic_index_in_dim(branch_gate.reshape(HEADS, HEAD_DIM), owner, 0)

    table = gathered(parts, 2 * tokens)
    table = table.reshape(-1, HEAD_DIM)

    steps = CHUNKS + (SECTIONS - 1) * DELAY
    sent = []
    result = done = None
    for step in range(steps):
        x = fresh[step] if step < DELAY else sent[step - DELAY]
        result, done = attend(step, places, info, x, gain, gate, table, done)
        if step + DELAY < steps:
            targets = SECTIONS if step < DELAY else SECTIONS - 1
            pairs = [(s, (s + 1) % SECTIONS) for s in range(targets)]
            sent.append(lax.ppermute(result, "section", pairs))
    groups = [
        [place * RINGS + row * 2 + c for place in range(depth) for row in (first, 3 - first)]
        for first in range(2)
        for c in range(2)
    ]
    done = lax.all_to_all(done, "seq", 0, 0, axis_index_groups=groups, tiled=True)
    done = done.reshape(HEADS, micro_count, patch_rows, HEAD_DIM).transpose(1, 2, 0, 3)
    return done.reshape(1, micro_count, patch_rows, channels)


def solution(mesh):
    return jax.shard_map(
        local,
        mesh=mesh,
        in_specs=(
            P(None, "seq", None),
            P("section", None, "seq", None),
            P("section", None, None, None),
            P("section", None),
            P("section", None),
            P("section", None),
        ),
        out_specs=P("section", None, "seq", None),
        check_vma=False,
    )
```

```python
import functools

import jax
import jax.numpy as jnp
from jax import lax
from jax.experimental import pallas as pl
from jax.experimental.pallas import tpu as pltpu
from jax.sharding import PartitionSpec as P

HEADS = 16
HEAD_DIM = 128
QUERY_BLOCK = 16
KEY_BLOCK = 32
SLOTS = 16
SECTIONS = 4
CHUNKS = 4
DELAY = 2
GROUP = 32
SPAN = SLOTS * KEY_BLOCK
SCORE_FLOOR = -1e30

RINGS = 8
SHIFTS = (0, 1, -1, 2, -2, 3, -3, 4)
FIRST, REST = (1, 2, 3, 4), (0, 5, 6, 7)
WAVES = ((0, 1, 2, 3), (4, 5, 6, 7))


def pack_kernel(cache, patches, *refs, shifts):
    outs, sems = refs[: len(shifts)], refs[-1]
    section, shard = lax.axis_index("section"), lax.axis_index("seq")
    z, upper = shard // RINGS, shard // 4 % 2
    tokens, channels = patches.shape
    chunk_tokens = outs[0].shape[1] - 2 * tokens
    token0 = pl.multiple_of((section ^ (section // 2)) * chunk_tokens, chunk_tokens)
    copies = []
    for k, shift in enumerate(shifts):
        for other in range(2):
            head = lax.rem(z + (shift + len(SHIFTS)), len(SHIFTS)) * 2 + (upper ^ other)
            key0 = pl.multiple_of(head * HEAD_DIM, HEAD_DIM)
            value0 = pl.multiple_of(channels + head * HEAD_DIM, HEAD_DIM)
            for which, (source, place, size) in enumerate(
                (
                    (cache.at[:, pl.ds(key0, HEAD_DIM)], 0, tokens),
                    (cache.at[:, pl.ds(value0, HEAD_DIM)], tokens, tokens),
                    (
                        patches.at[pl.ds(token0, chunk_tokens), pl.ds(key0, HEAD_DIM)],
                        2 * tokens,
                        chunk_tokens,
                    ),
                )
            ):
                copies.append(
                    pltpu.make_async_copy(
                        source, outs[k].at[other, pl.ds(place, size), :], sems.at[len(copies)]
                    )
                )
    for copy in copies:
        copy.start()
    for copy in copies:
        copy.wait()


def packed(cache, patches, shifts):
    tokens = patches.shape[0]
    piece = jax.ShapeDtypeStruct((2, 2 * tokens + tokens // CHUNKS, HEAD_DIM), jnp.bfloat16)
    count = len(shifts)
    return pl.pallas_call(
        functools.partial(pack_kernel, shifts=shifts),
        out_shape=(piece,) * count,
        in_specs=[pl.BlockSpec(memory_space=pltpu.HBM)] * 2,
        out_specs=(pl.BlockSpec(memory_space=pltpu.VMEM),) * count,
        scratch_shapes=[pltpu.SemaphoreType.DMA((count * 6,))],
        compiler_params=pltpu.CompilerParams(vmem_limit_bytes=61 * 1024 * 1024),
    )(cache, patches)


def part_kernel(*refs, count):
    own, others, sems = refs[count], refs[count + 1 : -1], refs[-1]
    copies = []
    for wave, other in zip(WAVES, others):
        for n, k in enumerate(wave):
            copies.append(pltpu.make_async_copy(refs[k].at[1], other.at[n], sems.at[0, k]))
            copies.append(
                pltpu.make_async_copy(
                    refs[k].at[0, pl.ds(0, own.shape[1]), :], own.at[k], sems.at[1, k]
                )
            )
    for copy in copies:
        copy.start()
    for copy in copies:
        copy.wait()


def parted(pieces, rows):
    count = len(pieces)
    own, *others = pl.pallas_call(
        functools.partial(part_kernel, count=count),
        out_shape=(
            jax.ShapeDtypeStruct((count, rows, HEAD_DIM), jnp.bfloat16),
            *(
                jax.ShapeDtypeStruct((len(wave), *pieces[0].shape[1:]), jnp.bfloat16)
                for wave in WAVES
            ),
        ),
        in_specs=[pl.BlockSpec(memory_space=pl.ANY)] * count,
        out_specs=(pl.BlockSpec(memory_space=pl.ANY),) * (1 + len(WAVES)),
        scratch_shapes=[pltpu.SemaphoreType.DMA((2, count))],
        compiler_params=pltpu.CompilerParams(vmem_limit_bytes=8 * 1024 * 1024),
    )(*pieces)
    return own, others


def arrange_kernel(info, *refs, skip):
    count = len(SHIFTS)
    pieces, crosses, out = refs[:count], refs[count:-1], refs[-1]
    z, upper = info[2], info[3]
    chunk_tokens = pieces[0].shape[1] - skip
    for wave, cross in zip(WAVES, crosses):
        for n, k in enumerate(wave):
            source = lax.rem(z + (count - SHIFTS[k]), count) * 2
            for part, index, lane in ((pieces[k], 0, upper), (cross, n, 1 - upper)):
                place = pl.multiple_of((source + lane) * chunk_tokens, chunk_tokens)
                out[pl.ds(place, chunk_tokens), :] = part[index, skip : skip + chunk_tokens, :]


def arranged(info, pieces, crosses, tokens, chunk_tokens):
    inputs = [*pieces, *crosses]
    rows = 2 * len(pieces) * chunk_tokens
    vmem = pl.BlockSpec(memory_space=pltpu.VMEM)
    return pl.pallas_call(
        functools.partial(arrange_kernel, skip=2 * tokens),
        out_shape=jax.ShapeDtypeStruct((rows, HEAD_DIM), jnp.bfloat16),
        in_specs=[pl.BlockSpec(memory_space=pltpu.SMEM)] + [vmem] * len(inputs),
        out_specs=vmem,
        compiler_params=pltpu.CompilerParams(vmem_limit_bytes=8 * 1024 * 1024),
    )(info, *inputs)


def gather_kernel(*refs, rows):
    parts, out, sems = refs[:-2], refs[-2], refs[-1]
    copies = []
    place = 0
    for n, part in enumerate(parts):
        size = part.shape[0]
        copies.append(
            pltpu.make_async_copy(
                part.at[:, pl.ds(0, rows), :], out.at[pl.ds(place, size)], sems.at[n]
            )
        )
        place += size
    for copy in copies:
        copy.start()
    for copy in copies:
        copy.wait()


def gathered(parts, rows):
    entries = sum(part.shape[0] for part in parts)
    return pl.pallas_call(
        functools.partial(gather_kernel, rows=rows),
        out_shape=jax.ShapeDtypeStruct((entries, rows, HEAD_DIM), jnp.bfloat16),
        in_specs=[pl.BlockSpec(memory_space=pl.ANY)] * len(parts),
        out_specs=pl.BlockSpec(memory_space=pltpu.VMEM),
        scratch_shapes=[pltpu.SemaphoreType.DMA((len(parts),))],
        compiler_params=pltpu.CompilerParams(vmem_limit_bytes=8 * 1024 * 1024),
    )(*parts)


def attend_kernel(places, info, x_ref, *refs, step):
    gain_ref, gate_ref, table = refs[:3]
    out_ref, done_ref = refs[-2:]
    section = info[0]
    chunk = step - section * DELAY
    live_keys = info[1] * KEY_BLOCK
    rows = out_ref.shape[0]
    chunk_tokens = done_ref.shape[1] // CHUNKS
    group_rows = GROUP * QUERY_BLOCK
    value_rows = done_ref.shape[1]
    group_sources = group_rows // chunk_tokens

    @pl.when((chunk >= 0) & (chunk < CHUNKS))
    def _():
        base = chunk * (rows // QUERY_BLOCK * SLOTS)
        token0 = pl.multiple_of(chunk * chunk_tokens, chunk_tokens)

        def one_group(index, carry):
            row0 = pl.multiple_of(index * group_rows, group_rows)
            here = pl.ds(row0, group_rows)
            wide = x_ref[here, :].astype(jnp.float32)
            mean = jnp.mean(wide * wide, axis=-1, keepdims=True)
            queries = (wide * lax.rsqrt(mean + 1e-06) * gain_ref[...]).astype(jnp.bfloat16)
            first = base + index * (GROUP * SLOTS)
            scores = []
            starts = []
            for g in range(GROUP):
                at = [
                    pl.multiple_of(places[first + g * SLOTS + j], KEY_BLOCK)
                    for j in range(SLOTS)
                ]
                starts.append(at)
                keys = jnp.concatenate(
                    [table[pl.ds(a, KEY_BLOCK), :] for a in at], axis=0
                )
                scores.append(
                    lax.dot_general(
                        queries[g * QUERY_BLOCK : (g + 1) * QUERY_BLOCK],
                        keys,
                        (((1,), (1,)), ((), ())),
                        preferred_element_type=jnp.float32,
                    )
                )
            scores = jnp.concatenate(scores, axis=0) * (HEAD_DIM**-0.5)
            lane = lax.broadcasted_iota(jnp.int32, scores.shape, 1)
            scores = jnp.where(lane < live_keys, scores, SCORE_FLOOR)
            highest = jnp.max(scores, axis=-1, keepdims=True)
            exponent = jnp.exp(scores - highest)
            total = jnp.sum(exponent, axis=-1, keepdims=True)
            weights = (exponent / total).astype(jnp.bfloat16)
            summed = []
            for g in range(GROUP):
                values = jnp.concatenate(
                    [table[pl.ds(a + value_rows, KEY_BLOCK), :] for a in starts[g]],
                    axis=0,
                )
                summed.append(
                    jnp.dot(
                        weights[g * QUERY_BLOCK : (g + 1) * QUERY_BLOCK],
                        values,
                        preferred_element_type=jnp.float32,
                    )
                )
            heads = jnp.concatenate(summed, axis=0).astype(jnp.bfloat16)
            updated = wide + gate_ref[...] * heads.astype(jnp.float32)
            updated = updated.astype(jnp.bfloat16)
            out_ref[here, :] = updated
            done_ref[pl.ds(index * group_sources, group_sources), pl.ds(token0, chunk_tokens), :] = (
                updated.reshape(group_sources, chunk_tokens, HEAD_DIM)
            )
            return carry

        lax.fori_loop(0, rows // group_rows, one_group, 0)

    if step < DELAY:

        @pl.when(section == SECTIONS - 1)
        def _():
            out_ref[...] = x_ref[...]


def attend(step, places, info, x, gain, gate, table, done):
    rows, width = x.shape
    vmem = pl.BlockSpec(memory_space=pltpu.VMEM)
    smem = pl.BlockSpec(memory_space=pltpu.SMEM)
    inputs = [places, info, x, gain, gate, table]
    aliases = {}
    done_shape = (CHUNKS * rows // HEADS // 8, HEADS * 8, width)
    if done is not None:
        aliases = {len(inputs): 1}
        inputs.append(done)
        done_shape = done.shape
    return pl.pallas_call(
        functools.partial(attend_kernel, step=step),
        out_shape=(
            jax.ShapeDtypeStruct((rows, width), jnp.bfloat16),
            jax.ShapeDtypeStruct(done_shape, jnp.bfloat16),
        ),
        in_specs=[smem, smem] + [vmem] * (len(inputs) - 2),
        out_specs=(vmem, vmem),
        input_output_aliases=aliases,
        compiler_params=pltpu.CompilerParams(vmem_limit_bytes=8 * 1024 * 1024),
        cost_estimate=pl.CostEstimate(
            flops=4 * rows * SPAN * HEAD_DIM,
            bytes_accessed=4 * rows * width,
            transcendentals=rows * SPAN,
        ),
    )(*inputs)


def merge_kernel(done, out, sems):
    copies = []
    for head in range(HEADS):
        lanes = pl.ds(head * HEAD_DIM, HEAD_DIM)
        copies.append(pltpu.make_async_copy(done.at[head], out.at[:, lanes], sems.at[head]))
    for copy in copies:
        copy.start()
    for copy in copies:
        copy.wait()


def merged(done):
    heads, tokens, width = done.shape
    space = pl.BlockSpec(memory_space=pl.ANY)
    return pl.pallas_call(
        merge_kernel,
        out_shape=jax.ShapeDtypeStruct((tokens, heads * width), jnp.bfloat16),
        in_specs=[space],
        out_specs=space,
        scratch_shapes=[pltpu.SemaphoreType.DMA((heads,))],
        compiler_params=pltpu.CompilerParams(vmem_limit_bytes=8 * 1024 * 1024),
    )(done)


def moved(value, rule):
    total = lax.axis_size("seq")
    pairs = []
    for place in range(total):
        z, y, core = place // RINGS, place // 2 % 4, place % 2
        z, y, core = rule(z, y, core)
        pairs.append((place, z % (total // RINGS) * RINGS + y * 2 + core))
    return lax.ppermute(value, "seq", pairs)


def across(value):
    return moved(value, lambda z, y, core: (z, 3 - y, core))


def beside(value):
    return moved(value, lambda z, y, core: (z, y ^ 1, core))


def twin(value):
    return moved(value, lambda z, y, core: (z, y, core ^ 1))


def local(patches, stale_cache, block_lists, block_counts, query_gain, branch_gate):
    section = lax.axis_index("section")
    shard = lax.axis_index("seq")
    depth = lax.axis_size("seq") // RINGS
    z, y, core = shard // RINGS, shard // 2 % 4, shard % 2
    upper = y // 2
    lane = jnp.minimum(y, 3 - y)
    owner = z * 2 + upper
    micro_count, patch_rows, channels = patches.shape
    sources = 2 * depth
    tokens = micro_count * patch_rows
    chunk_tokens = tokens // CHUNKS

    count = lax.dynamic_index_in_dim(block_counts[0], owner, 0, keepdims=False)
    info = jnp.stack([section, count, z, upper]).astype(jnp.int32)
    rows_in = (stale_cache.reshape(tokens, 2 * channels), patches.reshape(tokens, channels))
    pieces = [None] * depth
    for part in FIRST, REST:
        for k, piece in zip(part, packed(*rows_in, tuple(SHIFTS[k] for k in part))):
            pieces[k] = piece
    for k in range(1, len(SHIFTS)):
        shift = SHIFTS[k]
        pieces[k] = moved(pieces[k], lambda z, y, core: (z + shift, y, core))

    own, others = parted(pieces, 2 * tokens)
    own_beside = beside(own)
    crosses = [across(other) for other in others]
    cross = [value[:, : 2 * tokens] for value in crosses]
    parts = [own, own_beside, *cross, *(beside(value) for value in cross)]
    parts = parts + [twin(part) for part in parts]

    fresh = [arranged(info, pieces, crosses, tokens, chunk_tokens)]
    fresh.append(lax.ppermute(fresh[0], "section", [(1, 0), (2, 3)]))

    query_blocks = patch_rows // QUERY_BLOCK
    lists = lax.dynamic_index_in_dim(block_lists[0], owner, 0, keepdims=False)
    lists = lists.reshape(micro_count, depth, 4, 2, query_blocks, SLOTS)
    lists = lax.dynamic_index_in_dim(lists, core, 3, keepdims=False)
    lists = jnp.stack(
        [
            lax.dynamic_index_in_dim(lists, lane, 2, keepdims=False),
            lax.dynamic_index_in_dim(lists, 3 - lane, 2, keepdims=False),
        ],
        axis=2,
    )
    lists = lists.reshape(micro_count, sources, query_blocks, SLOTS).transpose(0, 2, 1, 3)
    lists = lists.reshape(CHUNKS, -1, sources, SLOTS).transpose(0, 2, 1, 3)
    per_shard = patch_rows // KEY_BLOCK
    per_micro = per_shard * depth * RINGS
    micro, rest = lists // per_micro, lists % per_micro
    holder, half = rest // per_shard, rest % per_shard
    back = (z + depth - holder // RINGS) % depth
    slot = jnp.where(back <= depth // 2, jnp.maximum(2 * back - 1, 0), 2 * (depth - back))
    row = holder // 2 % 4
    side = jnp.where(
        row == y, 0, jnp.where(row == (y ^ 1), 1, jnp.where(row == 3 - y, 2, 3))
    )
    entry = ((holder % 2 ^ core) * 4 + side) * depth + slot
    places = (entry * 2 * micro_count + micro) * patch_rows + half * KEY_BLOCK
    places = places.reshape(-1)
    gain = lax.dynamic_index_in_dim(query_gain.reshape(HEADS, HEAD_DIM), owner, 0)
    gate = lax.dynamic_index_in_dim(branch_gate.reshape(HEADS, HEAD_DIM), owner, 0)

    table = gathered(parts, 2 * tokens)
    table = table.reshape(-1, HEAD_DIM)

    steps = CHUNKS + (SECTIONS - 1) * DELAY
    sent = []
    result = done = None
    for step in range(steps):
        x = fresh[step] if step < DELAY else sent[step - DELAY]
        result, done = attend(step, places, info, x, gain, gate, table, done)
        if step + DELAY < steps:
            targets = SECTIONS if step < DELAY else SECTIONS - 1
            pairs = [(s, (s + 1) % SECTIONS) for s in range(targets)]
            sent.append(lax.ppermute(result, "section", pairs))
    groups = [
        [place * RINGS + row * 2 + c for place in range(depth) for row in (first, 3 - first)]
        for first in range(2)
        for c in range(2)
    ]
    done = lax.all_to_all(done, "seq", 0, 0, axis_index_groups=groups, tiled=True)
    return merged(done).reshape(1, micro_count, patch_rows, channels)


def solution(mesh):
    return jax.shard_map(
        local,
        mesh=mesh,
        in_specs=(
            P(None, "seq", None),
            P("section", None, "seq", None),
            P("section", None, None, None),
            P("section", None),
            P("section", None),
            P("section", None),
        ),
        out_specs=P("section", None, "seq", None),
        check_vma=False,
    )
```

```python
import functools

import jax
import jax.numpy as jnp
from jax import lax
from jax.experimental import pallas as pl
from jax.experimental.pallas import tpu as pltpu
from jax.sharding import PartitionSpec as P

HEADS = 16
HEAD_DIM = 128
QUERY_BLOCK = 16
KEY_BLOCK = 32
SLOTS = 16
SECTIONS = 4
CHUNKS = 4
DELAY = 2
GROUP = 32
SPAN = SLOTS * KEY_BLOCK
SCORE_FLOOR = -1e30

RINGS = 8
SHIFTS = (0, 1, -1, 2, -2, 3, -3, 4)
FIRST, REST = (1, 2, 3, 4), (0, 5, 6, 7)
WAVES = ((0, 1, 2, 3), (4, 5, 6, 7))


def pack_kernel(cache, patches, *refs, shifts):
    outs, sems = refs[: len(shifts)], refs[-1]
    section, shard = lax.axis_index("section"), lax.axis_index("seq")
    z, upper = shard // RINGS, shard // 4 % 2
    tokens, channels = patches.shape
    chunk_tokens = outs[0].shape[1] - 2 * tokens
    token0 = pl.multiple_of((section ^ (section // 2)) * chunk_tokens, chunk_tokens)
    copies = []
    for k, shift in enumerate(shifts):
        for other in range(2):
            head = lax.rem(z + (shift + len(SHIFTS)), len(SHIFTS)) * 2 + (upper ^ other)
            key0 = pl.multiple_of(head * HEAD_DIM, HEAD_DIM)
            value0 = pl.multiple_of(channels + head * HEAD_DIM, HEAD_DIM)
            for which, (source, place, size) in enumerate(
                (
                    (cache.at[:, pl.ds(key0, HEAD_DIM)], 0, tokens),
                    (cache.at[:, pl.ds(value0, HEAD_DIM)], tokens, tokens),
                    (
                        patches.at[pl.ds(token0, chunk_tokens), pl.ds(key0, HEAD_DIM)],
                        2 * tokens,
                        chunk_tokens,
                    ),
                )
            ):
                copies.append(
                    pltpu.make_async_copy(
                        source, outs[k].at[other, pl.ds(place, size), :], sems.at[len(copies)]
                    )
                )
    for copy in copies:
        copy.start()
    for copy in copies:
        copy.wait()


def packed(cache, patches, shifts):
    tokens = patches.shape[0]
    piece = jax.ShapeDtypeStruct((2, 2 * tokens + tokens // CHUNKS, HEAD_DIM), jnp.bfloat16)
    count = len(shifts)
    return pl.pallas_call(
        functools.partial(pack_kernel, shifts=shifts),
        out_shape=(piece,) * count,
        in_specs=[pl.BlockSpec(memory_space=pltpu.HBM)] * 2,
        out_specs=(pl.BlockSpec(memory_space=pltpu.VMEM),) * count,
        scratch_shapes=[pltpu.SemaphoreType.DMA((count * 6,))],
        compiler_params=pltpu.CompilerParams(vmem_limit_bytes=61 * 1024 * 1024),
    )(cache, patches)


def part_kernel(*refs, count):
    own, others, sems = refs[count], refs[count + 1 : -1], refs[-1]
    copies = []
    for wave, other in zip(WAVES, others):
        for n, k in enumerate(wave):
            copies.append(pltpu.make_async_copy(refs[k].at[1], other.at[n], sems.at[0, k]))
            copies.append(
                pltpu.make_async_copy(
                    refs[k].at[0, pl.ds(0, own.shape[1]), :], own.at[k], sems.at[1, k]
                )
            )
    for copy in copies:
        copy.start()
    for copy in copies:
        copy.wait()


def parted(pieces, rows):
    count = len(pieces)
    own, *others = pl.pallas_call(
        functools.partial(part_kernel, count=count),
        out_shape=(
            jax.ShapeDtypeStruct((count, rows, HEAD_DIM), jnp.bfloat16),
            *(
                jax.ShapeDtypeStruct((len(wave), *pieces[0].shape[1:]), jnp.bfloat16)
                for wave in WAVES
            ),
        ),
        in_specs=[pl.BlockSpec(memory_space=pl.ANY)] * count,
        out_specs=(pl.BlockSpec(memory_space=pl.ANY),) * (1 + len(WAVES)),
        scratch_shapes=[pltpu.SemaphoreType.DMA((2, count))],
        compiler_params=pltpu.CompilerParams(vmem_limit_bytes=8 * 1024 * 1024),
    )(*pieces)
    return own, others


def arrange_kernel(info, *refs, skip):
    count = len(SHIFTS)
    pieces, crosses, out = refs[:count], refs[count:-1], refs[-1]
    z, upper = info[2], info[3]
    chunk_tokens = pieces[0].shape[1] - skip
    for wave, cross in zip(WAVES, crosses):
        for n, k in enumerate(wave):
            source = lax.rem(z + (count - SHIFTS[k]), count) * 2
            for part, index, lane in ((pieces[k], 0, upper), (cross, n, 1 - upper)):
                place = pl.multiple_of((source + lane) * chunk_tokens, chunk_tokens)
                out[pl.ds(place, chunk_tokens), :] = part[index, skip : skip + chunk_tokens, :]


def arranged(info, pieces, crosses, tokens, chunk_tokens):
    inputs = [*pieces, *crosses]
    rows = 2 * len(pieces) * chunk_tokens
    vmem = pl.BlockSpec(memory_space=pltpu.VMEM)
    return pl.pallas_call(
        functools.partial(arrange_kernel, skip=2 * tokens),
        out_shape=jax.ShapeDtypeStruct((rows, HEAD_DIM), jnp.bfloat16),
        in_specs=[pl.BlockSpec(memory_space=pltpu.SMEM)] + [vmem] * len(inputs),
        out_specs=vmem,
        compiler_params=pltpu.CompilerParams(vmem_limit_bytes=8 * 1024 * 1024),
    )(info, *inputs)


def gather_kernel(*refs, rows):
    parts, out, sems = refs[:-2], refs[-2], refs[-1]
    copies = []
    place = 0
    for n, part in enumerate(parts):
        size = part.shape[0]
        copies.append(
            pltpu.make_async_copy(
                part.at[:, pl.ds(0, rows), :], out.at[pl.ds(place, size)], sems.at[n]
            )
        )
        place += size
    for copy in copies:
        copy.start()
    for copy in copies:
        copy.wait()


def gathered(parts, rows):
    entries = sum(part.shape[0] for part in parts)
    return pl.pallas_call(
        functools.partial(gather_kernel, rows=rows),
        out_shape=jax.ShapeDtypeStruct((entries, rows, HEAD_DIM), jnp.bfloat16),
        in_specs=[pl.BlockSpec(memory_space=pl.ANY)] * len(parts),
        out_specs=pl.BlockSpec(memory_space=pltpu.VMEM),
        scratch_shapes=[pltpu.SemaphoreType.DMA((len(parts),))],
        compiler_params=pltpu.CompilerParams(vmem_limit_bytes=8 * 1024 * 1024),
    )(*parts)


def attend_kernel(places, info, x_ref, *refs, step):
    gain_ref, gate_ref, table = refs[:3]
    out_ref, done_ref = refs[-2:]
    section = info[0]
    chunk = step - section * DELAY
    live_keys = info[1] * KEY_BLOCK
    rows = out_ref.shape[0]
    chunk_tokens = done_ref.shape[1] // CHUNKS
    group_rows = GROUP * QUERY_BLOCK
    value_rows = done_ref.shape[1]
    group_sources = group_rows // chunk_tokens

    @pl.when((chunk >= 0) & (chunk < CHUNKS))
    def _():
        base = chunk * (rows // QUERY_BLOCK * SLOTS)
        token0 = pl.multiple_of(chunk * chunk_tokens, chunk_tokens)

        def one_group(index, carry):
            row0 = pl.multiple_of(index * group_rows, group_rows)
            here = pl.ds(row0, group_rows)
            wide = x_ref[here, :].astype(jnp.float32)
            mean = jnp.mean(wide * wide, axis=-1, keepdims=True)
            queries = (wide * lax.rsqrt(mean + 1e-06) * gain_ref[...]).astype(jnp.bfloat16)
            first = base + index * (GROUP * SLOTS)
            scores = []
            starts = []
            for g in range(GROUP):
                at = [
                    pl.multiple_of(places[first + g * SLOTS + j], KEY_BLOCK)
                    for j in range(SLOTS)
                ]
                starts.append(at)
                keys = jnp.concatenate(
                    [table[pl.ds(a, KEY_BLOCK), :] for a in at], axis=0
                )
                scores.append(
                    lax.dot_general(
                        queries[g * QUERY_BLOCK : (g + 1) * QUERY_BLOCK],
                        keys,
                        (((1,), (1,)), ((), ())),
                        preferred_element_type=jnp.float32,
                    )
                )
            scores = jnp.concatenate(scores, axis=0)
            lane = lax.broadcasted_iota(jnp.int32, scores.shape, 1)
            scores = jnp.where(lane < live_keys, scores, SCORE_FLOOR)
            highest = jnp.max(scores, axis=-1, keepdims=True)
            exponent = jnp.exp((scores - highest) * (HEAD_DIM**-0.5))
            total = jnp.sum(exponent, axis=-1, keepdims=True)
            weights = (exponent * (1.0 / total)).astype(jnp.bfloat16)
            summed = []
            for g in range(GROUP):
                values = jnp.concatenate(
                    [table[pl.ds(a + value_rows, KEY_BLOCK), :] for a in starts[g]],
                    axis=0,
                )
                summed.append(
                    jnp.dot(
                        weights[g * QUERY_BLOCK : (g + 1) * QUERY_BLOCK],
                        values,
                        preferred_element_type=jnp.float32,
                    )
                )
            heads = jnp.concatenate(summed, axis=0).astype(jnp.bfloat16)
            updated = wide + gate_ref[...] * heads.astype(jnp.float32)
            updated = updated.astype(jnp.bfloat16)
            out_ref[here, :] = updated
            done_ref[pl.ds(index * group_sources, group_sources), pl.ds(token0, chunk_tokens), :] = (
                updated.reshape(group_sources, chunk_tokens, HEAD_DIM)
            )
            return carry

        lax.fori_loop(0, rows // group_rows, one_group, 0)

    if step < DELAY:

        @pl.when(section == SECTIONS - 1)
        def _():
            out_ref[...] = x_ref[...]


def attend(step, places, info, x, gain, gate, table, done):
    rows, width = x.shape
    vmem = pl.BlockSpec(memory_space=pltpu.VMEM)
    smem = pl.BlockSpec(memory_space=pltpu.SMEM)
    inputs = [places, info, x, gain, gate, table]
    aliases = {}
    done_shape = (CHUNKS * rows // HEADS // 8, HEADS * 8, width)
    if done is not None:
        aliases = {len(inputs): 1}
        inputs.append(done)
        done_shape = done.shape
    return pl.pallas_call(
        functools.partial(attend_kernel, step=step),
        out_shape=(
            jax.ShapeDtypeStruct((rows, width), jnp.bfloat16),
            jax.ShapeDtypeStruct(done_shape, jnp.bfloat16),
        ),
        in_specs=[smem, smem] + [vmem] * (len(inputs) - 2),
        out_specs=(vmem, vmem),
        input_output_aliases=aliases,
        compiler_params=pltpu.CompilerParams(vmem_limit_bytes=8 * 1024 * 1024),
        cost_estimate=pl.CostEstimate(
            flops=4 * rows * SPAN * HEAD_DIM,
            bytes_accessed=4 * rows * width,
            transcendentals=rows * SPAN,
        ),
    )(*inputs)


def merge_kernel(done, out, sems):
    copies = []
    for head in range(HEADS):
        lanes = pl.ds(head * HEAD_DIM, HEAD_DIM)
        copies.append(pltpu.make_async_copy(done.at[head], out.at[:, lanes], sems.at[head]))
    for copy in copies:
        copy.start()
    for copy in copies:
        copy.wait()


def merged(done):
    heads, tokens, width = done.shape
    space = pl.BlockSpec(memory_space=pl.ANY)
    return pl.pallas_call(
        merge_kernel,
        out_shape=jax.ShapeDtypeStruct((tokens, heads * width), jnp.bfloat16),
        in_specs=[space],
        out_specs=space,
        scratch_shapes=[pltpu.SemaphoreType.DMA((heads,))],
        compiler_params=pltpu.CompilerParams(vmem_limit_bytes=8 * 1024 * 1024),
    )(done)


def moved(value, rule):
    total = lax.axis_size("seq")
    pairs = []
    for place in range(total):
        z, y, core = place // RINGS, place // 2 % 4, place % 2
        z, y, core = rule(z, y, core)
        pairs.append((place, z % (total // RINGS) * RINGS + y * 2 + core))
    return lax.ppermute(value, "seq", pairs)


def across(value):
    return moved(value, lambda z, y, core: (z, 3 - y, core))


def beside(value):
    return moved(value, lambda z, y, core: (z, y ^ 1, core))


def twin(value):
    return moved(value, lambda z, y, core: (z, y, core ^ 1))


def local(patches, stale_cache, block_lists, block_counts, query_gain, branch_gate):
    section = lax.axis_index("section")
    shard = lax.axis_index("seq")
    depth = lax.axis_size("seq") // RINGS
    z, y, core = shard // RINGS, shard // 2 % 4, shard % 2
    upper = y // 2
    lane = jnp.minimum(y, 3 - y)
    owner = z * 2 + upper
    micro_count, patch_rows, channels = patches.shape
    sources = 2 * depth
    tokens = micro_count * patch_rows
    chunk_tokens = tokens // CHUNKS

    count = lax.dynamic_index_in_dim(block_counts[0], owner, 0, keepdims=False)
    info = jnp.stack([section, count, z, upper]).astype(jnp.int32)
    rows_in = (stale_cache.reshape(tokens, 2 * channels), patches.reshape(tokens, channels))
    pieces = [None] * depth
    for part in FIRST, REST:
        for k, piece in zip(part, packed(*rows_in, tuple(SHIFTS[k] for k in part))):
            pieces[k] = piece
    for k in range(1, len(SHIFTS)):
        shift = SHIFTS[k]
        pieces[k] = moved(pieces[k], lambda z, y, core: (z + shift, y, core))

    own, others = parted(pieces, 2 * tokens)
    own_beside = beside(own)
    crosses = [across(other) for other in others]
    cross = [value[:, : 2 * tokens] for value in crosses]
    parts = [own, own_beside, *cross, *(beside(value) for value in cross)]
    parts = parts + [twin(part) for part in parts]

    fresh = [arranged(info, pieces, crosses, tokens, chunk_tokens)]
    fresh.append(lax.ppermute(fresh[0], "section", [(1, 0), (2, 3)]))

    query_blocks = patch_rows // QUERY_BLOCK
    lists = lax.dynamic_index_in_dim(block_lists[0], owner, 0, keepdims=False)
    lists = lists.reshape(micro_count, depth, 4, 2, query_blocks, SLOTS)
    lists = lax.dynamic_index_in_dim(lists, core, 3, keepdims=False)
    lists = jnp.stack(
        [
            lax.dynamic_index_in_dim(lists, lane, 2, keepdims=False),
            lax.dynamic_index_in_dim(lists, 3 - lane, 2, keepdims=False),
        ],
        axis=2,
    )
    lists = lists.reshape(micro_count, sources, query_blocks, SLOTS).transpose(0, 2, 1, 3)
    lists = lists.reshape(CHUNKS, -1, sources, SLOTS).transpose(0, 2, 1, 3)
    per_shard = patch_rows // KEY_BLOCK
    per_micro = per_shard * depth * RINGS
    micro, rest = lists // per_micro, lists % per_micro
    holder, half = rest // per_shard, rest % per_shard
    back = (z + depth - holder // RINGS) % depth
    slot = jnp.where(back <= depth // 2, jnp.maximum(2 * back - 1, 0), 2 * (depth - back))
    row = holder // 2 % 4
    side = jnp.where(
        row == y, 0, jnp.where(row == (y ^ 1), 1, jnp.where(row == 3 - y, 2, 3))
    )
    entry = ((holder % 2 ^ core) * 4 + side) * depth + slot
    places = (entry * 2 * micro_count + micro) * patch_rows + half * KEY_BLOCK
    places = places.reshape(-1)
    gain = lax.dynamic_index_in_dim(query_gain.reshape(HEADS, HEAD_DIM), owner, 0)
    gate = lax.dynamic_index_in_dim(branch_gate.reshape(HEADS, HEAD_DIM), owner, 0)

    table = gathered(parts, 2 * tokens)
    table = table.reshape(-1, HEAD_DIM)

    steps = CHUNKS + (SECTIONS - 1) * DELAY
    sent = []
    result = done = None
    for step in range(steps):
        x = fresh[step] if step < DELAY else sent[step - DELAY]
        result, done = attend(step, places, info, x, gain, gate, table, done)
        if step + DELAY < steps:
            targets = SECTIONS if step < DELAY else SECTIONS - 1
            pairs = [(s, (s + 1) % SECTIONS) for s in range(targets)]
            sent.append(lax.ppermute(result, "section", pairs))
    groups = [
        [place * RINGS + row * 2 + c for place in range(depth) for row in (first, 3 - first)]
        for first in range(2)
        for c in range(2)
    ]
    done = lax.all_to_all(done, "seq", 0, 0, axis_index_groups=groups, tiled=True)
    return merged(done).reshape(1, micro_count, patch_rows, channels)


def solution(mesh):
    return jax.shard_map(
        local,
        mesh=mesh,
        in_specs=(
            P(None, "seq", None),
            P("section", None, "seq", None),
            P("section", None, None, None),
            P("section", None),
            P("section", None),
            P("section", None),
        ),
        out_specs=P("section", None, "seq", None),
        check_vma=False,
    )
```
